512 devices in a mesh: llm: 16 (over z), enc: 32 (over y, x, core).
Axes of the slice: x: 4, y: 4, z: 16, core: 2. Of those that a mesh axis runs over, the one named last changes fastest.
Arguments:
- frame_counts: int32 [16, 2], P('llm'), may hold values from 1 to 2048, as said below
- dest_rank: int32 [16, 2048, 2, 1], P('llm', 'enc'), may hold values from 0 to 15; in each aligned block of 128 rows (0 to 127, 128 to 255, ..., all dimensions but the last counted through in order) at most 12 rows name the same one
- grad_rows: bfloat16 [16, 16, 384, 2048], P('llm', None, 'enc'), may hold values from -6 to 6
- queries: bfloat16 [16, 2048, 2, 640], P('llm', 'enc'), may hold values from -200 to 200
- key_rows: bfloat16 [16, 2048, 2, 640], P('llm', 'enc'), may hold values from -5 to 5
- value_rows: bfloat16 [16, 2048, 2, 640], P('llm', 'enc'), may hold values from -6 to 6
- conv2_pre: bfloat16 [16, 2048, 2, 640], P('llm', 'enc'), may hold values from -6 to 6
- conv1_pre: bfloat16 [16, 4096, 2, 640], P('llm', 'enc'), may hold values from -6 to 6
- norm_gain: float32 [640], replicated, may hold values from 0.25 to 1.75
- w_proj: bfloat16 [640, 2048], P(None, 'llm'), may hold values from -0.125 to 0.125
- w_out: bfloat16 [640, 640], P('llm'), may hold values from -0.25 to 0.25
- w_qkv: bfloat16 [3, 640, 640], P(None, 'llm'), may hold values from -0.25 to 0.25
- w_conv2: bfloat16 [3, 640, 640], P(None, 'llm'), may hold values from -0.125 to 0.125
- w_conv1: bfloat16 [3, 128, 640], P(None, 'llm'), may hold values from -0.125 to 0.125
Outputs:
- mel_grad: float32 [16, 4096, 2, 128], P('llm', 'enc')
The draws below stay inside these ranges and needn't reach their ends.
Inputs may be any that keep to these rules, and one draw needn't show every extreme that they name: `dest_rank`: in the 128 frames of one device block of one group, at most 12 name the same LLM rank, a bound that some block reaches. `frame_counts`: in each group one clip, drawn at random, has all 2048 frames.
All inputs are finite; a program needn't handle non-finite values.
Results may differ from the reference program's by a relative error of at most 0.012.
Values may be sent and summed in bfloat16 or wider, within the bound.
A program may use at most 64 MiB of HBM per device.

```python
import math
import jax
import jax.numpy as jnp
import numpy as np
from jax import lax

HID = 2048
HEADS = 16
HEAD_DIM = 40
MEL = 128
D = 640
FR_DEV = 64
CLIPS = 2
GROUPS = 16
LENGTH = 2048
CAP = 12
SLOTS = 384
N_ENC = 32


def shared_base(key):
    return jnp.clip(jax.random.normal(key, (GROUPS, LENGTH, CLIPS, D), jnp.float32), -5.0, 5.0)


def draw_frame_counts(key, part):
    key = jax.random.fold_in(key, 5)
    first, second = jax.random.split(key)
    others = jax.random.randint(first, (GROUPS, CLIPS), LENGTH // 4, LENGTH + 1)
    full_clip = jax.random.randint(second, (GROUPS,), 0, CLIPS)
    clip_ids = jnp.arange(CLIPS)
    counts = jnp.where(clip_ids[None, :] == full_clip[:, None], LENGTH, others)
    return counts.astype(jnp.int32)


def draw_key_rows(key, part):
    base = shared_base(key)
    return base.astype(jnp.bfloat16)


def draw_queries(key, part):
    key = jax.random.fold_in(key, 7)
    own = 3.5 * jnp.clip(jax.random.normal(key, (GROUPS, LENGTH, CLIPS, D), jnp.float32), -5.0, 5.0)
    return own.astype(jnp.bfloat16)


def level_of(rng, dims, cuts, least, top_value):
    gain = 1.0
    for position, shards_of in cuts:
        steps = jax.random.uniform(jax.random.fold_in(jax.random.fold_in(rng, 6), position), (shards_of,), jnp.float32, least / len(cuts), top_value / len(cuts))
        gain = gain * jnp.repeat(jnp.exp(steps), dims[position] // shards_of).reshape((-1,) + (1,) * (len(dims) - 1 - position))
    return gain


def routed_block(key, own, number, rows, amount, top, reach, lean):
    ranking = jax.random.permutation(key, amount)
    packed, ordinary = portions_of(amount, rows * top, reach, lean, True), portions_of(amount, rows * top, reach, lean, False)
    places = jnp.arange(amount)

    def named(lengths, rotation):
        used = int((lengths > 0).sum())
        fixed = max(1, used // 4)
        passed = fixed + (places - fixed + rotation * (used - fixed)) % max(1, amount - fixed)
        return jnp.zeros((amount,), jnp.int32).at[ranking[jnp.where(places < fixed, places, passed)]].set(jnp.asarray(lengths, jnp.int32))

    lengths = jnp.where(number % 4 == 0, named(packed, number // 4), named(ordinary, number - number // 4 - 1))
    mixed = jax.random.permutation(jax.random.fold_in(own, 3), amount)
    donor, taker = mixed[0:amount // 2 * 2:2], mixed[1:amount // 2 * 2:2]
    margin = jnp.minimum(lengths[donor] - 1, reach - lengths[taker]) // 2
    margin = jnp.where((donor == ranking[0]) | (taker == ranking[0]) | (lengths[taker] == 0), 0, jnp.maximum(margin, 0))
    passed = jax.random.randint(jax.random.fold_in(own, 4), (amount // 2,), 0, 1 << 20) % (margin + 1)
    lengths = lengths.at[donor].add(-passed).at[taker].add(passed)
    members = jnp.searchsorted(jnp.cumsum(lengths), jnp.arange(rows * top), side="right").astype(jnp.int32)
    grid = members.reshape(top, rows).T
    grid = grid[jax.random.permutation(jax.random.fold_in(own, 1), rows)]
    rotation = jax.random.randint(jax.random.fold_in(own, 2), (rows, 1), 0, top)
    return jnp.take_along_axis(grid, (jnp.arange(top)[None, :] + rotation) % top, axis=1)


def portions_of(count, total, reach, slope, full):
    weights = [(1 << 20) // math.isqrt(grade ** slope) + 1 for grade in range(1, count + 1)]
    largest = reach if full else min(reach, max(-(-total // count), total * weights[0] // sum(weights)))
    least = 1 if total - largest >= count - 1 else 0
    given, spare = [largest] + [least] * (count - 1), total - largest - least * (count - 1)
    while spare > 0:
        candidates = [i for i in range(1, count) if given[i] < largest] or [i for i in range(1, count) if given[i] < reach]
        mass, budget = sum([weights[i] for i in candidates]), spare
        for i in candidates:
            extra = min(reach - given[i], max(1, budget * weights[i] // mass), spare)
            given[i] = given[i] + extra
            spare = spare - extra
    return np.array(given)


def scatter_about(stream_key, shape, scale, bound, cuts=(), dtype=jnp.bfloat16):
    values = jax.random.normal(stream_key, shape, jnp.float32) * scale
    if len(cuts) > 0:
        values = level_of(stream_key, shape, cuts, -0.22, 0.18) * values
    return jnp.clip(values, min=-bound, max=bound).astype(dtype)


def setup_inputs(seed: int = 0) -> dict:
    seeds = jax.random.split(jax.random.key(seed), 15)
    frame_counts = draw_frame_counts(jax.random.fold_in(seeds[14], 71), 0)
    dest_rank_keys = jax.random.split(jax.random.fold_in(seeds[1], 1), GROUPS * LENGTH * CLIPS // (FR_DEV * CLIPS))
    dest_rank_turns = jax.random.permutation(jax.random.fold_in(seeds[1], 3), GROUPS * LENGTH * CLIPS // (FR_DEV * CLIPS))
    dest_rank = jax.vmap(lambda own, number: routed_block(jax.random.fold_in(seeds[1], 2), own, number, FR_DEV * CLIPS, GROUPS, 1, CAP, 1))(dest_rank_keys, dest_rank_turns).reshape((GROUPS, LENGTH, CLIPS, 1))
    grad_rows = scatter_about(seeds[2], (GROUPS, GROUPS, SLOTS, HID), 1.0, 6.0, ((0, 16), (2, 32)))
    queries = draw_queries(jax.random.fold_in(seeds[14], 71), 0)
    key_rows = draw_key_rows(jax.random.fold_in(seeds[14], 71), 0)
    value_rows = scatter_about(seeds[5], (GROUPS, LENGTH, CLIPS, D), 1.0, 6.0, ((0, 16), (1, 32)))
    conv2_pre = scatter_about(seeds[6], (GROUPS, LENGTH, CLIPS, D), 1.0, 6.0, ((0, 16), (1, 32)))
    conv1_pre = scatter_about(seeds[7], (GROUPS, 2 * LENGTH, CLIPS, D), 1.0, 6.0, ((0, 16), (1, 32)))
    norm_gain = jnp.clip(1.0 + 0.15 * jax.random.normal(seeds[8], (D,), jnp.float32), 0.25, 1.75)
    w_proj = scatter_about(seeds[9], (D, HID), HID ** -0.5, 0.125, ((1, 16),))
    w_out = scatter_about(seeds[10], (D, D), D ** -0.5, 0.25, ((0, 16),))
    w_qkv = scatter_about(seeds[11], (3, D, D), D ** -0.5, 0.25, ((1, 16),))
    w_conv2 = scatter_about(seeds[12], (3, D, D), (3 * D) ** -0.5, 0.125, ((1, 16),))
    w_conv1 = scatter_about(seeds[13], (3, MEL, D), (3 * D) ** -0.5, 0.125, ((1, 16),))
    return dict(frame_counts=frame_counts, dest_rank=dest_rank, grad_rows=grad_rows, queries=queries, key_rows=key_rows, value_rows=value_rows, conv2_pre=conv2_pre, conv1_pre=conv1_pre, norm_gain=norm_gain, w_proj=w_proj, w_out=w_out, w_qkv=w_qkv, w_conv2=w_conv2, w_conv1=w_conv1)


inv_root_two = 0.7071067811865476
inv_root_two_pi = 0.3989422804014327

def gelu_value(value):
    return value * 0.5 * (1.0 + lax.erf(value * inv_root_two))

def gelu_slope(value):
    return 0.5 * (1.0 + lax.erf(value * inv_root_two)) + value * jnp.exp(-0.5 * value * value) * inv_root_two_pi

def positional(places, width):
    halfwidth = width // 2
    ladder = jnp.arange(halfwidth).astype(jnp.float32)
    inverse = jnp.exp(-jnp.log(jnp.float32(10000.0)) * ladder / (halfwidth - 1))
    angle = places.astype(jnp.float32)[:, None] * inverse[None, :]
    return jnp.concatenate([jnp.sin(angle), jnp.cos(angle)], axis=-1)

def attend(query, keyed, valued, d_out, keep):
    scale = HEAD_DIM ** (-0.5)
    length = query.shape[0]
    pairs = query.shape[1]
    depth = query.shape[2]
    block = math.gcd(length, 512)
    count = length // block
    keyed_f = keyed.astype(jnp.float32)
    valued_f = valued.astype(jnp.float32)
    query_blocks = query.astype(jnp.float32).reshape(count, block, pairs, depth)
    d_blocks = d_out.astype(jnp.float32).reshape(count, block, pairs, depth)

    def step(carry, pieces):
        key_acc, value_acc = carry
        query_f, d_out_f = pieces
        scores = jnp.einsum('qnd,knd->nqk', query_f, keyed_f) * scale
        scores = jnp.where(keep[:, None, :], scores, jnp.float32(-jnp.inf))
        highest = lax.optimization_barrier(jnp.max(scores, axis=-1, keepdims=True))
        weights = jnp.exp(scores - highest)
        probs = weights / lax.optimization_barrier(jnp.sum(weights, axis=-1, keepdims=True))
        probs_b = probs.astype(jnp.bfloat16).astype(jnp.float32)
        attn_o = jnp.einsum('nqk,knd->qnd', probs_b, valued_f)
        delta = lax.optimization_barrier(jnp.sum(d_out_f * attn_o, axis=-1))
        value_acc = value_acc + jnp.einsum('nqk,qnd->knd', probs_b, d_out_f)
        d_probs = jnp.einsum('qnd,knd->nqk', d_out_f, valued_f)
        d_scores = (probs * (d_probs - jnp.transpose(delta)[:, :, None]) * scale).astype(jnp.bfloat16).astype(jnp.float32)
        d_query = jnp.einsum('nqk,knd->qnd', d_scores, keyed_f).astype(jnp.bfloat16)
        key_acc = key_acc + jnp.einsum('nqk,qnd->knd', d_scores, query_f)
        return ((key_acc, value_acc), d_query)
    zeros = jnp.zeros((length, pairs, depth), jnp.float32)
    (key_acc, value_acc), d_query = lax.scan(step, (zeros, zeros), (query_blocks, d_blocks))
    return (d_query.reshape(length, pairs, depth), key_acc.astype(jnp.bfloat16), value_acc.astype(jnp.bfloat16))

def reference(frame_counts, dest_rank, grad_rows, queries, key_rows, value_rows, conv2_pre, conv1_pre, norm_gain, w_proj, w_out, w_qkv, w_conv2, w_conv1):
    width = HEADS * HEAD_DIM
    block = FR_DEV * CLIPS

    def one_group(group):
        counts = lax.dynamic_index_in_dim(frame_counts, group, 0, keepdims=False)
        target_all = lax.dynamic_index_in_dim(dest_rank, group, 0, keepdims=False)[:, :, 0]
        held_rows = lax.dynamic_index_in_dim(grad_rows, group, 1, keepdims=False)
        valid = jnp.arange(LENGTH).astype(jnp.int32)[:, None] < counts[None, :]
        valid_blocks = valid.reshape(N_ENC, block)
        target = target_all.reshape(N_ENC, block)
        onehot = ((target[:, :, None] == jnp.arange(GROUPS).astype(jnp.int32)[None, None, :]) & valid_blocks[:, :, None]).astype(jnp.int32)
        running = jnp.cumsum(onehot, axis=1)
        ranks = lax.optimization_barrier(jnp.sum(running * onehot, axis=-1)) - 1
        starts = (jnp.arange(N_ENC).astype(jnp.int32) * CAP)[:, None]
        slot = jnp.where(valid_blocks, target * SLOTS + starts + ranks, 0).reshape(-1).astype(jnp.int32)
        picked = jnp.take(held_rows.reshape(-1, HID), slot, axis=0)
        picked = picked * valid.reshape(-1)[:, None].astype(jnp.bfloat16)
        upstream = jnp.dot(picked, jnp.transpose(w_proj), preferred_element_type=jnp.float32).astype(jnp.bfloat16)
        d_attn = jnp.dot(upstream, jnp.transpose(w_out), preferred_element_type=jnp.float32).astype(jnp.bfloat16)
        pairs = CLIPS * HEADS
        query = lax.dynamic_index_in_dim(queries, group, 0, keepdims=False).reshape(LENGTH, pairs, HEAD_DIM)
        keyed = lax.dynamic_index_in_dim(key_rows, group, 0, keepdims=False).reshape(LENGTH, pairs, HEAD_DIM)
        valued = lax.dynamic_index_in_dim(value_rows, group, 0, keepdims=False).reshape(LENGTH, pairs, HEAD_DIM)
        d_out = d_attn.reshape(LENGTH, pairs, HEAD_DIM)
        keep = jnp.transpose(jnp.repeat(valid, HEADS, axis=1))
        d_query, d_key, d_value = attend(query, keyed, valued, d_out, keep)
        stacked = jnp.stack([d_query.reshape(LENGTH * CLIPS, width), d_key.reshape(LENGTH * CLIPS, width), d_value.reshape(LENGTH * CLIPS, width)], axis=1).astype(jnp.float32)
        d_normed = jnp.einsum('fjo,jio->fi', stacked, w_qkv.astype(jnp.float32)).reshape(LENGTH, CLIPS, width)
        pre_two = lax.dynamic_index_in_dim(conv2_pre, group, 0, keepdims=False).astype(jnp.float32)
        table = positional(jnp.arange(LENGTH).astype(jnp.int32), width)
        layer_in = gelu_value(pre_two) + table[:, None, :]
        center = lax.optimization_barrier(jnp.mean(layer_in, axis=-1, keepdims=True))
        spread = lax.optimization_barrier(jnp.mean((layer_in - center) ** 2, axis=-1, keepdims=True))
        rstd = 1.0 / jnp.sqrt(spread + 1e-05)
        normed = (layer_in - center) * rstd
        scaled = d_normed * norm_gain
        d_layer = rstd * (scaled - lax.optimization_barrier(jnp.mean(scaled, axis=-1, keepdims=True)) - normed * lax.optimization_barrier(jnp.mean(scaled * normed, axis=-1, keepdims=True)))
        d_conv2 = ((upstream.astype(jnp.float32).reshape(LENGTH, CLIPS, width) + d_layer) * gelu_slope(pre_two)).astype(jnp.bfloat16)
        taps = jnp.einsum('tco,kio->ktci', d_conv2.astype(jnp.float32), w_conv2.astype(jnp.float32))
        zero_row = jnp.zeros((1, CLIPS, width), jnp.float32)
        even = taps[1]
        odd = taps[2] + jnp.concatenate([taps[0][1:], zero_row], axis=0)
        d_hidden = jnp.stack([even, odd], axis=1).reshape(2 * LENGTH, CLIPS, width)
        pre_one = lax.dynamic_index_in_dim(conv1_pre, group, 0, keepdims=False).astype(jnp.float32)
        d_conv1 = (d_hidden * gelu_slope(pre_one)).astype(jnp.bfloat16)
        mel_taps = jnp.einsum('sci,kmi->kscm', d_conv1.astype(jnp.float32), w_conv1.astype(jnp.float32))
        zero_mel = jnp.zeros((1, CLIPS, MEL), jnp.float32)
        after = jnp.concatenate([mel_taps[0][1:], zero_mel], axis=0)
        before = jnp.concatenate([zero_mel, mel_taps[2][:-1]], axis=0)
        return after + mel_taps[1] + before
    return lax.map(one_group, jnp.arange(GROUPS).astype(jnp.int32))
```

```python
import functools

import jax
import jax.numpy as jnp
import numpy as np
from jax import lax
from jax.experimental import pallas as pl
from jax.experimental.pallas import tpu as pltpu
from jax.sharding import PartitionSpec as P

MESH = pl.DeviceIdType.MESH
F32, BF16 = jnp.float32, jnp.bfloat16
HEAD_DIM = 40
WIDTH = 640
HID = 2048
LENGTH = 2048
SCALE = HEAD_DIM ** (-0.5)
LOG2E = 1.4426950408889634
MASKED = -1e30
ROOT_HALF = 0.7071067811865476
INV_ROOT_TWO_PI = 0.3989422804014327
QB = 256


def gelu_value(value):
    return value * 0.5 * (1.0 + lax.erf(value * ROOT_HALF))


def gelu_slope(value):
    return (
        0.5 * (1.0 + lax.erf(value * ROOT_HALF))
        + value * jnp.exp(-0.5 * value * value) * INV_ROOT_TWO_PI
    )


def dot(a, b, dims):
    return lax.dot_general(a, b, (dims, ((), ())), preferred_element_type=F32)


NN = ((1,), (0,))
NT = ((1,), (1,))
TN = ((0,), (0,))


def tables():
    inverse = 10000.0 ** (-np.arange(320) / 319.0)
    base = 128.0 * np.arange(16)[:, None] * inverse[None, :]
    local = np.arange(128.0)[:, None] * inverse[None, :]
    first = np.concatenate([np.sin(base), np.cos(base)], axis=1)
    second = np.concatenate([np.cos(base), -np.sin(base)], axis=1)
    chip = np.stack([first, second], axis=1).astype(np.float32)
    near = np.stack(
        [np.concatenate([np.cos(local)] * 2, 1), np.concatenate([np.sin(local)] * 2, 1)]
    ).astype(np.float32)
    return chip, near


def kernel(
    counts, target, grads, q_in, k_in, v_in, c2_in, c1_in, gain, wp_in, wo_in, wqkv_in, wc2_in, wc1_in,
    chip_tab, near_tab,
    out,
    g_loc, q_loc, k_loc, v_loc, c2_loc, c1_loc, wo_loc, wqkv_loc, wc2_loc, wc1_loc, near,
    w_slab, wp, wr, w_full, w_last,
    cl1, cl2, xb1, xb2, head_send, qkv, kn, vn, qn,
    u_send, u_recv, up_send, up, d_send, d_out, dn,
    e_mat, big, rl, dk_acc, dv_acc, grad_t, grad_recv,
    slope1, halo1, d2_buf, halo2, mel_buf, mel_recv,
    loc_sem, wpz_s, wpz_r, wp1_s, wp1_r, wp2_s, wp2_r, wpc_s, wpc_r,
    wrz_s, wrz_r, wr1_s, wr1_r, wr2_s, wr2_r, wrc_s, wrc_r,
    xs, xr, qs, qr, us, ur, ds_, dr, bs, br, hs, hr,
):
    z = lax.axis_index("llm")
    e = lax.axis_index("enc")
    core = lax.rem(e, 2)
    other = 1 - core
    chip = e // 2
    x = lax.rem(chip, 4)
    y = chip // 4
    a = jnp.where(core == 0, x, y)
    b = jnp.where(core == 0, y, x)
    sibling = (z, chip * 2 + other)

    def along_a(step):
        to = lax.rem(a + step, 4)
        return (z, jnp.where(core == 0, y * 4 + to, to * 4 + x) * 2 + core)

    def along_b(step):
        to = lax.rem(b + step, 4)
        return (z, jnp.where(core == 0, to * 4 + x, y * 4 + to) * 2 + core)

    def on_chip(number):
        return (z, number * 2 + core)

    def remote(src, dst, send, recv, device):
        return pltpu.make_async_remote_copy(
            src_ref=src, dst_ref=dst, send_sem=send, recv_sem=recv, device_id=device, device_id_type=MESH
        )

    loads = [
        (q_in.at[0], q_loc), (k_in.at[0], k_loc), (v_in.at[0], v_loc), (wo_in, wo_loc), (wqkv_in, wqkv_loc),
        (wc2_in, wc2_loc), (wc1_in, wc1_loc), (c2_in.at[0], c2_loc), (c1_in.at[0], c1_loc),
        (grads, g_loc), (near_tab, near),
    ]
    for i, (src, dst) in enumerate(loads):
        pltpu.make_async_copy(src, dst, loc_sem.at[i]).start()

    def loaded(i):
        pltpu.make_async_copy(loads[i][0], loads[i][1], loc_sem.at[i]).wait()

    barrier = pltpu.get_barrier_semaphore()

    def greet(step, carry):
        pl.semaphore_signal(barrier, inc=1, device_id=(lax.rem(z + step, 16), e), device_id_type=MESH)
        pl.semaphore_signal(
            barrier, inc=1, device_id=on_chip(lax.rem(chip + step, 16)), device_id_type=MESH
        )
        return carry

    lax.fori_loop(1, 16, greet, 0)
    pl.semaphore_signal(barrier, inc=1, device_id=sibling, device_id_type=MESH)
    pl.semaphore_wait(barrier, 31)

    piece = 2 * b + a // 2
    kind = lax.rem(a, 2) + 2 * core
    wp_rows = pl.ds(pl.multiple_of(piece * 80, 16), 80)

    def wpz(step, index):
        return remote(
            wp_in.at[wp_rows, :],
            wp.at[wp_rows, pl.ds(pl.multiple_of((kind * 4 + index) * 128, 128), 128)],
            wpz_s.at[step], wpz_r.at[index], (lax.rem(z + step, 16), e),
        )

    wp_sends = lax.rem(z, 4) == kind
    wp_own = pltpu.make_async_copy(
        wp_in.at[wp_rows, :],
        wp.at[wp_rows, pl.ds(pl.multiple_of((kind * 4 + z // 4) * 128, 128), 128)],
        loc_sem.at[11],
    )

    @pl.when(wp_sends)
    def _():
        def body(step, carry):
            wpz(step, z // 4).start()
            return carry

        lax.fori_loop(1, 16, body, 0)
        wp_own.start()

    for i, ref in enumerate((q_loc, k_loc, v_loc)):
        loaded(i)
        for clip in range(2):
            cl1[clip, i * 64 : (i + 1) * 64, :] = ref[:, clip, :]
    swap1 = remote(cl1.at[other], xb1.at[core], xs.at[0], xr.at[0], sibling)
    swap1.start()
    keep1 = pltpu.make_async_copy(cl1.at[core], xb1.at[core], loc_sem.at[12])
    keep1.start()

    for i in range(3, 7):
        loaded(i)
    parts = [wo_loc[...].astype(F32)]
    parts += [wqkv_loc[i].astype(F32) for i in range(3)]
    parts += [wc2_loc[i].astype(F32) for i in range(3)]
    parts += [wc1_loc[i].astype(F32) for i in range(3)]
    parts += [jnp.zeros((16, WIDTH), F32)]
    w_slab[...] = jnp.concatenate(parts, axis=0).astype(BF16)
    group8 = a + 4 * core
    wr_rows = pl.ds(pl.multiple_of(b * 80, 16), 80)

    def wrz(step, index):
        return remote(
            w_slab.at[wr_rows, :], wr.at[group8 * 2 + index, wr_rows, :],
            wrz_s.at[step], wrz_r.at[index], (lax.rem(z + step, 16), e),
        )

    wr_sends = lax.rem(z, 8) == group8
    wr_own = pltpu.make_async_copy(
        w_slab.at[wr_rows, :], wr.at[group8 * 2 + z // 8, wr_rows, :], loc_sem.at[13]
    )

    @pl.when(wr_sends)
    def _():
        def body(step, carry):
            wrz(step, z // 8).start()
            return carry

        lax.fori_loop(1, 16, body, 0)
        wr_own.start()

    for index in range(4):
        @pl.when(kind + 4 * index != z)
        def _():
            wpz(1, index).wait_recv()

    @pl.when(wp_sends)
    def _():
        wp_own.wait()

    def wp1(step):
        block = wp.at[wp_rows, pl.ds(pl.multiple_of(kind * 512, 128), 512)]
        return remote(block, block, wp1_s.at[step], wp1_r.at[step], along_a(step))

    for step in range(1, 4):
        wp1(step).start()

    swap1.wait_recv()
    keep1.wait()
    places = chip * 128 + lax.broadcasted_iota(jnp.int32, (8, 128), 1)
    row8 = lax.broadcasted_iota(jnp.int32, (8, 128), 0)
    own_count = jnp.where(core == 0, counts[0, 0], counts[0, 1])
    ones_rows = jnp.where(row8 == 0, 1.0, 0.0)
    bias_rows = jnp.where((row8 == 0) & (places >= own_count), MASKED, 0.0)
    zero_rows = jnp.zeros((8, 128), F32)
    for i, extra in enumerate((ones_rows, bias_rows, zero_rows)):
        rows = jnp.concatenate(
            [xb1[0, i * 64 : (i + 1) * 64, :], xb1[1, i * 64 : (i + 1) * 64, :]], axis=0
        ).astype(F32)
        turned = jnp.transpose(rows)
        for head in range(16):
            head_send[head, i * 48 : (i + 1) * 48, :] = jnp.concatenate(
                [turned[head * 40 : head * 40 + 40], extra], axis=0
            ).astype(BF16)
    chip_lanes = pl.ds(pl.multiple_of(chip * 128, 128), 128)

    def qkv_copy(step):
        to = lax.rem(chip + step, 16)
        return remote(head_send.at[to], qkv.at[:, chip_lanes], qs.at[step], qr.at[step], on_chip(to))

    def start_qkv(step, carry):
        qkv_copy(step).start()
        return carry

    lax.fori_loop(1, 16, start_qkv, 0)
    qkv_own = pltpu.make_async_copy(head_send.at[chip], qkv.at[:, chip_lanes], loc_sem.at[14])
    qkv_own.start()

    for step in range(1, 4):
        wp1(step).wait_recv()

    def wp_set(number):
        return wp.at[
            pl.ds(pl.multiple_of(number * 160, 16), 160), pl.ds(pl.multiple_of(core * 1024, 128), 1024)
        ]

    def wp2(step):
        return remote(wp_set(b), wp_set(b), wp2_s.at[step], wp2_r.at[step], along_b(step))

    def wpc(step):
        held = wp_set(lax.rem(b - step + 4, 4))
        return remote(held, held, wpc_s.at[step], wpc_r.at[step], sibling)

    for step in range(1, 4):
        wp2(step).start()
    wpc(0).start()

    loaded(7)
    loaded(8)
    for clip in range(2):
        cl2[clip, 0:64, :] = c2_loc[:, clip, :]
        cl2[clip, 64:192, :] = c1_loc[:, clip, :]
    swap2 = remote(cl2.at[other], xb2.at[core], xs.at[1], xr.at[1], sibling)
    swap2.start()
    keep2 = pltpu.make_async_copy(cl2.at[core], xb2.at[core], loc_sem.at[15])
    keep2.start()

    for index in range(2):
        @pl.when(group8 + 8 * index != z)
        def _():
            wrz(1, index).wait_recv()

    @pl.when(wr_sends)
    def _():
        wr_own.wait()

    def wr1(step):
        block = wr.at[pl.ds(group8 * 2, 2), wr_rows, :]
        return remote(block, block, wr1_s.at[step], wr1_r.at[step], along_a(step))

    for step in range(1, 4):
        wr1(step).start()

    for step in range(1, 4):
        wp2(step).wait_recv()
        wpc(step).start()

    loaded(9)
    for step in range(4):
        wpc(step).wait_recv()

    total = jnp.zeros((192, WIDTH), F32)
    for number in range(4):
        rows = jnp.concatenate(
            [g_loc[:, (number + 4 * i) * 128 : (number + 4 * i + 1) * 128] for i in range(4)], axis=1
        )
        total = total + dot(rows, wp[:, number * 512 : (number + 1) * 512], NT)
    slot_row = lax.broadcasted_iota(jnp.int32, (256, 192), 0)
    held_row = lax.broadcasted_iota(jnp.int32, (256, 192), 1)
    order = (lax.rem(slot_row, 16) * 16 + slot_row // 16 == held_row).astype(F32).astype(BF16)
    u_send[...] = dot(order, total.astype(BF16), NN).astype(BF16).reshape(16, 16, WIDTH)

    def u_copy(step):
        to = lax.rem(z + step, 16)
        return remote(u_send.at[to], u_recv.at[z], us.at[step], ur.at[step], (to, e))

    def start_u(step, carry):
        u_copy(step).start()
        return carry

    lax.fori_loop(1, 16, start_u, 0)
    u_own = pltpu.make_async_copy(u_send.at[z], u_recv.at[z], loc_sem.at[16])
    u_own.start()

    for step in range(1, 4):
        wr1(step).wait_recv()

    def wr_set(number):
        return wr.at[pl.ds(core * 8, 8), pl.ds(pl.multiple_of(number * 80, 16), 80), :]

    def wr2(step):
        return remote(wr_set(b), wr_set(b), wr2_s.at[step], wr2_r.at[step], along_b(step))

    def wrc(step):
        held = wr_set(lax.rem(b - step + 4, 4))
        return remote(held, held, wrc_s.at[step], wrc_r.at[step], sibling)

    for step in range(1, 4):
        wr2(step).start()
    wrc(0).start()

    swap2.wait_recv()
    keep2.wait()
    after = on_chip(lax.rem(chip + 1, 16))
    before = on_chip(lax.rem(chip + 15, 16))
    edge_up = remote(xb2.at[1, pl.ds(176, 16), :], halo1.at[0], hs.at[0], hr.at[0], after)
    edge_down = remote(xb2.at[0, pl.ds(64, 16), :], halo1.at[1], hs.at[1], hr.at[1], before)
    edge_up.start()
    edge_down.start()

    def wait_qkv(step, carry):
        qkv_copy(step).wait_recv()
        return carry

    lax.fori_loop(1, 16, wait_qkv, 0)
    qkv_own.wait()
    qn[...] = jnp.transpose(qkv[0:48, :].astype(F32)).astype(BF16)
    kn[...] = jnp.transpose(qkv[48:96, :].astype(F32)).astype(BF16)
    vn[...] = jnp.transpose(qkv[96:144, :].astype(F32)).astype(BF16)

    def exponentials(number, carry):
        lanes = pl.ds(pl.multiple_of(number * QB, QB), QB)
        big[...] = dot(kn[...], qkv[0:48, lanes], NN)
        highest = jnp.max(big[...], axis=0, keepdims=True)
        weights = jnp.exp2((big[...] - highest) * (SCALE * LOG2E))
        e_mat[:, lanes] = weights.astype(BF16)
        rl[:, lanes] = 1.0 / jnp.sum(weights, axis=0, keepdims=True)
        return carry

    lax.fori_loop(0, LENGTH // QB, exponentials, 0)

    for step in range(1, 4):
        wr2(step).wait_recv()
        wrc(step).start()
    for step in range(4):
        wrc(step).wait_recv()

    def compact(number, carry):
        first = 2 * number
        slabs = []
        for place in (first, first + 1):
            slabs.append(wr[lax.rem(place, 8) * 2 + place // 8].astype(F32))
        rows = pl.ds(pl.multiple_of(number * 80, 16), 80)
        for i in range(7):
            w_full[i, rows, :] = jnp.concatenate(
                [slab[i * 40 : i * 40 + 40] for slab in slabs], axis=0
            ).astype(BF16)
        for i in range(3):
            w_last[pl.ds(pl.multiple_of(i * 128 + number * 16, 16), 16), :] = jnp.concatenate(
                [slab[280 + i * 8 : 288 + i * 8] for slab in slabs], axis=0
            ).astype(BF16)
        return carry

    lax.fori_loop(0, 8, compact, 0)

    slots = lax.broadcasted_iota(jnp.int32, (256, 64), 0)
    frame = e * 64 + lax.broadcasted_iota(jnp.int32, (256, 64), 1)
    named = []
    for clip in range(2):
        hit = (target[clip : clip + 1, :] == slots // 16) & (frame < counts[0, clip])
        named.append(jnp.where(hit, 1.0, 0.0))
    earlier = lax.broadcasted_iota(jnp.int32, (64, 64), 0)
    later = lax.broadcasted_iota(jnp.int32, (64, 64), 1)
    upto = (earlier <= later).astype(F32).astype(BF16)
    under = (earlier < later).astype(F32).astype(BF16)
    named_b = [part.astype(BF16) for part in named]
    seen = [
        dot(named_b[0], upto, NN) + dot(named_b[1], under, NN),
        dot(named_b[0], upto, NN) + dot(named_b[1], upto, NN),
    ]
    within = lax.rem(slots, 16).astype(F32) + 1.0
    choose = jnp.concatenate(
        [jnp.where(seen[i] == within, named[i], 0.0) for i in range(2)], axis=1
    ).astype(BF16)

    def wait_u(step, carry):
        u_copy(step).wait_recv()
        return carry

    lax.fori_loop(1, 16, wait_u, 0)
    u_own.wait()
    up_send[...] = (
        dot(choose, u_recv[...].reshape(256, WIDTH), TN).astype(BF16).reshape(2, 64, WIDTH)
    )
    swap3 = remote(up_send.at[other], up.at[core], xs.at[2], xr.at[2], sibling)
    swap3.start()
    keep3 = pltpu.make_async_copy(up_send.at[core], up.at[core], loc_sem.at[17])
    keep3.start()
    swap3.wait_recv()
    keep3.wait()
    d_attn = dot(w_full[0], up[...].reshape(128, WIDTH), NT)
    for head in range(16):
        d_send[head] = jnp.concatenate([d_attn[head * 40 : head * 40 + 40], zero_rows], axis=0).astype(
            BF16
        )

    def d_copy(step):
        to = lax.rem(chip + step, 16)
        return remote(d_send.at[to], d_out.at[:, chip_lanes], ds_.at[step], dr.at[step], on_chip(to))

    def start_d(step, carry):
        d_copy(step).start()
        return carry

    lax.fori_loop(1, 16, start_d, 0)
    d_own = pltpu.make_async_copy(d_send.at[chip], d_out.at[:, chip_lanes], loc_sem.at[18])
    d_own.start()

    edge_up.wait_recv()
    edge_down.wait_recv()
    for i in range(5):
        lanes = slice(i * 128, i * 128 + 128)
        slope1[i, 0:16, :] = gelu_slope(halo1[0, :, lanes].astype(F32))
        slope1[i, 16:144, :] = gelu_slope(xb2[0, 64:192, lanes].astype(F32))
        slope1[i, 144:272, :] = gelu_slope(xb2[1, 64:192, lanes].astype(F32))
        slope1[i, 272:288, :] = gelu_slope(halo1[1, :, lanes].astype(F32))

    def wait_d(step, carry):
        d_copy(step).wait_recv()
        return carry

    lax.fori_loop(1, 16, wait_d, 0)
    d_own.wait()
    shared = d_out[...].astype(F32) * rl[...]
    d_out[...] = shared.astype(BF16)
    dn[...] = jnp.transpose(shared).astype(BF16)
    dk_acc[...] = jnp.zeros_like(dk_acc)
    dv_acc[...] = jnp.zeros_like(dv_acc)

    def gradients(number, carry):
        lanes = pl.ds(pl.multiple_of(number * QB, QB), QB)
        weights = e_mat[:, lanes]
        big[...] = dot(vn[...], d_out[:, lanes], NN)
        delta = jnp.sum(weights.astype(F32) * big[...], axis=0, keepdims=True) * rl[:, lanes]
        slopes = (weights.astype(F32) * (big[...] - delta)).astype(BF16)
        dv_acc[...] += dot(weights, dn[lanes, :], NN)
        dk_acc[...] += dot(slopes, qn[lanes, :], NN)
        grad_t[0:48, lanes] = (dot(qkv[48:96, :], slopes, NN) * SCALE).astype(BF16)
        return carry

    lax.fori_loop(0, LENGTH // QB, gradients, 0)
    grad_t[48:96, :] = jnp.transpose(dk_acc[...] * SCALE).astype(BF16)
    grad_t[96:144, :] = jnp.transpose(dv_acc[...]).astype(BF16)

    def grad_lanes(number):
        return grad_t.at[:, pl.ds(pl.multiple_of(number * 128, 128), 128)]

    def b_copy(step):
        to = lax.rem(chip + step, 16)
        return remote(grad_lanes(to), grad_recv.at[chip], bs.at[step], br.at[step], on_chip(to))

    def start_b(step, carry):
        b_copy(step).start()
        return carry

    lax.fori_loop(1, 16, start_b, 0)
    b_own = pltpu.make_async_copy(grad_lanes(chip), grad_recv.at[chip], loc_sem.at[19])
    b_own.start()

    loaded(10)
    pre_two = jnp.concatenate([xb2[0, 0:64, :], xb2[1, 0:64, :]], axis=0).astype(F32)
    pair = chip_tab[chip]
    layer_in = gelu_value(pre_two) + pair[0:1] * near[0] + pair[1:2] * near[1]
    center = jnp.mean(layer_in, axis=-1, keepdims=True)
    moved = layer_in - center
    rstd = 1.0 / jnp.sqrt(jnp.mean(moved * moved, axis=-1, keepdims=True) + 1e-05)
    normed = moved * rstd

    def wait_b(step, carry):
        b_copy(step).wait_recv()
        return carry

    lax.fori_loop(1, 16, wait_b, 0)
    b_own.wait()
    d_normed = jnp.zeros((128, WIDTH), F32)
    for i in range(3):
        turned = jnp.concatenate(
            [grad_recv[head, i * 48 : i * 48 + 48, :].astype(F32)[0:40] for head in range(16)], axis=0
        )
        d_normed = d_normed + dot(jnp.transpose(turned).astype(BF16), w_full[1 + i], NT)
    scaled = d_normed * gain[...]
    d_layer = rstd * (
        scaled
        - jnp.mean(scaled, axis=-1, keepdims=True)
        - normed * jnp.mean(scaled * normed, axis=-1, keepdims=True)
    )
    d2_buf[...] = (
        (up[...].reshape(128, WIDTH).astype(F32) + d_layer) * gelu_slope(pre_two)
    ).astype(BF16)
    row_up = remote(d2_buf.at[pl.ds(112, 16), :], halo2.at[0], hs.at[2], hr.at[2], after)
    row_down = remote(d2_buf.at[pl.ds(0, 16), :], halo2.at[1], hs.at[3], hr.at[3], before)
    row_up.start()
    row_down.start()
    row_up.wait_recv()
    row_down.wait_recv()
    has_before = jnp.where(chip > 0, 1.0, 0.0).astype(BF16)
    has_after = jnp.where(chip < 15, 1.0, 0.0).astype(BF16)
    rows = jnp.concatenate([halo2[0] * has_before, d2_buf[...], halo2[1] * has_after], axis=0)
    tap0, tap1, tap2 = (dot(rows, w_full[4 + i], NT) for i in range(3))
    even_slope = jnp.concatenate([slope1[i, pl.ds(16, 136, stride=2), :] for i in range(5)], axis=1)
    odd_slope = jnp.concatenate([slope1[i, pl.ds(1, 136, stride=2), :] for i in range(5)], axis=1)
    spot = lax.broadcasted_iota(jnp.int32, (136, 1), 0)
    even = tap1[16:152] * even_slope
    even = jnp.where((spot < 128) | (chip < 15), even, 0.0).astype(BF16)
    odd = (tap2[8:144] + tap0[9:145]) * odd_slope
    odd = jnp.where((spot >= 8) | (chip > 0), odd, 0.0).astype(BF16)
    even_mel = dot(even, w_last[...], NT)
    odd_mel = dot(odd, w_last[...], NT)
    mel_even = odd_mel[8:136, 0:128] + even_mel[0:128, 128:256] + odd_mel[7:135, 256:384]
    mel_odd = even_mel[1:129, 0:128] + odd_mel[8:136, 128:256] + even_mel[0:128, 256:384]
    for block in range(2):
        mel_buf[block, 0:64, :] = mel_even[block * 64 : block * 64 + 64]
        mel_buf[block, 64:128, :] = mel_odd[block * 64 : block * 64 + 64]
    swap4 = remote(mel_buf.at[other], mel_recv, xs.at[3], xr.at[3], sibling)
    swap4.start()
    out[core] = mel_buf[core]
    swap4.wait_recv()
    out[other] = mel_recv[...]

    @pl.when(wp_sends)
    def _():
        def body(step, carry):
            wpz(step, z // 4).wait_send()
            return carry

        lax.fori_loop(1, 16, body, 0)

    @pl.when(wr_sends)
    def _():
        def body(step, carry):
            wrz(step, z // 8).wait_send()
            return carry

        lax.fori_loop(1, 16, body, 0)

    for step in range(1, 4):
        for copy in (wp1, wp2, wpc, wr1, wr2, wrc):
            copy(step).wait_send()
    wpc(0).wait_send()
    wrc(0).wait_send()

    def sent(step, carry):
        for copy in (qkv_copy, u_copy, d_copy, b_copy):
            copy(step).wait_send()
        return carry

    lax.fori_loop(1, 16, sent, 0)
    for copy in (swap1, swap2, swap3, swap4, edge_up, edge_down, row_up, row_down):
        copy.wait_send()


def per_device(
    frame_counts, dest_rank, grad_rows, queries, key_rows, value_rows, conv2_pre, conv1_pre,
    norm_gain, w_proj, w_out, w_qkv, w_conv2, w_conv1,
):
    chip_tab, near_tab = tables()
    target = jnp.transpose(dest_rank[0, :, :, 0])
    grads = jnp.transpose(grad_rows[0], (1, 0, 2)).reshape(192, HID)
    anywhere = pl.BlockSpec(memory_space=pl.ANY)
    vmem = pl.BlockSpec(memory_space=pltpu.VMEM)
    scratch = [
        ((192, HID), BF16), ((64, 2, WIDTH), BF16), ((64, 2, WIDTH), BF16), ((64, 2, WIDTH), BF16),
        ((64, 2, WIDTH), BF16), ((128, 2, WIDTH), BF16), ((40, WIDTH), BF16), ((3, 40, WIDTH), BF16),
        ((3, 40, WIDTH), BF16), ((3, 8, WIDTH), BF16), ((2, 128, WIDTH), F32),
        ((320, WIDTH), BF16), ((WIDTH, HID), BF16), ((16, 320, WIDTH), BF16), ((7, WIDTH, WIDTH), BF16),
        ((384, WIDTH), BF16),
        ((2, 192, WIDTH), BF16), ((2, 192, WIDTH), BF16), ((2, 192, WIDTH), BF16), ((2, 192, WIDTH), BF16),
        ((16, 144, 128), BF16), ((144, LENGTH), BF16), ((LENGTH, 48), BF16), ((LENGTH, 48), BF16),
        ((LENGTH, 48), BF16),
        ((16, 16, WIDTH), BF16), ((16, 16, WIDTH), BF16), ((2, 64, WIDTH), BF16), ((2, 64, WIDTH), BF16),
        ((16, 48, 128), BF16), ((48, LENGTH), BF16), ((LENGTH, 48), BF16),
        ((LENGTH, LENGTH), BF16), ((LENGTH, QB), F32), ((1, LENGTH), F32), ((LENGTH, 48), F32),
        ((LENGTH, 48), F32), ((144, LENGTH), BF16), ((16, 144, 128), BF16),
        ((5, 288, 128), F32), ((2, 16, WIDTH), BF16), ((128, WIDTH), BF16), ((2, 16, WIDTH), BF16),
        ((2, 128, 128), F32), ((128, 128), F32),
    ]
    sems = [20, 16, 4, 4, 4, 4, 4, 4, 4, 16, 2, 4, 4, 4, 4, 4, 4, 4, 4, 16, 16, 16, 16, 16, 16, 16, 16, 4, 4]
    result = pl.pallas_call(
        kernel,
        out_shape=jax.ShapeDtypeStruct((2, 128, 128), F32),
        in_specs=[pl.BlockSpec(memory_space=pltpu.SMEM), vmem]
        + [anywhere] * 6 + [vmem] + [anywhere] * 5 + [vmem, anywhere],
        out_specs=vmem,
        scratch_shapes=[pltpu.VMEM(shape, kind) for shape, kind in scratch]
        + [pltpu.SemaphoreType.DMA((n,)) for n in sems],
        compiler_params=pltpu.CompilerParams(
            collective_id=0, has_side_effects=True, vmem_limit_bytes=58 << 20
        ),
    )(
        frame_counts, target, grads, queries, key_rows, value_rows, conv2_pre, conv1_pre,
        norm_gain.reshape(1, WIDTH), w_proj, w_out, w_qkv, w_conv2, w_conv1,
        jnp.asarray(chip_tab), jnp.asarray(near_tab),
    )
    mel = result.reshape(2, 2, 64, 128)
    return jnp.transpose(mel, (2, 1, 0, 3)).reshape(1, 128, 2, 128)


def solution(mesh):
    rows = P("llm", "enc", None, None)
    placed = (
        P("llm", None), rows, P("llm", None, "enc", None), rows, rows, rows, rows, rows, P(),
        P(None, "llm"), P("llm", None), P(None, "llm", None), P(None, "llm", None), P(None, "llm", None),
    )
    return jax.shard_map(
        per_device, mesh=mesh, in_specs=placed, out_specs=rows, check_vma=False
    )
```

```python
import functools

import jax
import jax.numpy as jnp
import numpy as np
from jax import lax
from jax.experimental import pallas as pl
from jax.experimental.pallas import tpu as pltpu
from jax.sharding import PartitionSpec as P

MESH = pl.DeviceIdType.MESH
F32, BF16 = jnp.float32, jnp.bfloat16
HEAD_DIM = 40
WIDTH = 640
HID = 2048
LENGTH = 2048
SCALE = HEAD_DIM ** (-0.5)
LOG2E = 1.4426950408889634
MASKED = -1e30
ROOT_HALF = 0.7071067811865476
INV_ROOT_TWO_PI = 0.3989422804014327
QB = 512


def gelu_value(value):
    return value * 0.5 * (1.0 + lax.erf(value * ROOT_HALF))


def gelu_slope(value):
    return (
        0.5 * (1.0 + lax.erf(value * ROOT_HALF))
        + value * jnp.exp(-0.5 * value * value) * INV_ROOT_TWO_PI
    )


def dot(a, b, dims):
    return lax.dot_general(a, b, (dims, ((), ())), preferred_element_type=F32)


NN = ((1,), (0,))
NT = ((1,), (1,))
TN = ((0,), (0,))


def tables():
    inverse = 10000.0 ** (-np.arange(320) / 319.0)
    base = 128.0 * np.arange(16)[:, None] * inverse[None, :]
    local = np.arange(128.0)[:, None] * inverse[None, :]
    first = np.concatenate([np.sin(base), np.cos(base)], axis=1)
    second = np.concatenate([np.cos(base), -np.sin(base)], axis=1)
    chip = np.stack([first, second], axis=1).astype(np.float32)
    near = np.stack(
        [np.concatenate([np.cos(local)] * 2, 1), np.concatenate([np.sin(local)] * 2, 1)]
    ).astype(np.float32)
    return chip, near


def kernel(
    counts, target_in, grads, q_in, k_in, v_in, c2_in, c1_in, gain_in, wp_in, wo_in, wqkv_in, wc2_in, wc1_in,
    chip_tab, near_tab,
    out,
    target, gain, pair, g_loc, q_loc, k_loc, v_loc, c2_loc, c1_loc, wo_loc, wqkv_loc, wc2_loc, wc1_loc, near,
    a_slab, b_slab, wp, wa, wb, w_full, w_last,
    cl1, cl2, xb1, xb2, head_send, qkv, qt, kt, vt, kn, vn, qn,
    u_send, u_recv, up_send, up, d_send, d_out, dn,
    e_mat, big, rl, delta, attn, dk_acc, dv_acc, dq_t, dkv_t, dq_recv, dkv_recv,
    slope1, halo1, d2_buf, halo2, mel_buf, mel_recv,
    loc_sem, wpz_s, wpz_r, wp1_s, wp1_r, wp2_s, wp2_r, wpc_s, wpc_r,
    waz_s, waz_r, wa1_s, wa1_r, wa2_s, wa2_r, wac_s, wac_r,
    wbz_s, wbz_r, wb1_s, wb1_r, wb2_s, wb2_r, wbc_s, wbc_r,
    xs, xr, qs, qr, us, ur, ds_, dr, bs, br, cs, cr, hs, hr,
):
    z = lax.axis_index("llm")
    e = lax.axis_index("enc")
    core = lax.rem(e, 2)
    other = 1 - core
    chip = e // 2
    x = lax.rem(chip, 4)
    y = chip // 4
    a = jnp.where(core == 0, x, y)
    b = jnp.where(core == 0, y, x)
    sibling = (z, chip * 2 + other)

    def along_a(step):
        to = lax.rem(a + step, 4)
        return (z, jnp.where(core == 0, y * 4 + to, to * 4 + x) * 2 + core)

    def along_b(step):
        to = lax.rem(b + step, 4)
        return (z, jnp.where(core == 0, to * 4 + x, y * 4 + to) * 2 + core)

    def along_z(step):
        return (lax.rem(z + step, 16), e)

    def on_chip(number):
        return (z, number * 2 + core)

    def remote(src, dst, send, recv, device):
        return pltpu.make_async_remote_copy(
            src_ref=src, dst_ref=dst, send_sem=send, recv_sem=recv, device_id=device, device_id_type=MESH
        )

    def each(low, high, act):
        def body(step, carry):
            act(step)
            return carry

        lax.fori_loop(low, high, body, 0)

    barrier = pltpu.get_barrier_semaphore()

    def greet(step):
        pl.semaphore_signal(barrier, inc=1, device_id=along_z(step), device_id_type=MESH)
        pl.semaphore_signal(
            barrier, inc=1, device_id=on_chip(lax.rem(chip + step, 16)), device_id_type=MESH
        )

    each(1, 16, greet)
    pl.semaphore_signal(barrier, inc=1, device_id=sibling, device_id_type=MESH)

    loads = [
        (q_in.at[0], q_loc), (k_in.at[0], k_loc), (v_in.at[0], v_loc), (wo_in, wo_loc), (wc1_in, wc1_loc),
        (wqkv_in, wqkv_loc), (wc2_in, wc2_loc), (c2_in.at[0], c2_loc), (c1_in.at[0], c1_loc),
        (grads, g_loc), (near_tab, near), (target_in, target), (gain_in, gain), (chip_tab.at[chip], pair),
    ]
    for i, (src, dst) in enumerate(loads):
        pltpu.make_async_copy(src, dst, loc_sem.at[i]).start()

    def loaded(i):
        pltpu.make_async_copy(loads[i][0], loads[i][1], loc_sem.at[i]).wait()

    pl.semaphore_wait(barrier, 31)

    piece = 2 * b + a // 2
    kind = lax.rem(a, 2) + 2 * core
    wp_rows = pl.ds(pl.multiple_of(piece * 80, 16), 80)

    def wpz(step, index):
        return remote(
            wp_in.at[wp_rows, :],
            wp.at[wp_rows, pl.ds(pl.multiple_of((kind * 4 + index) * 128, 128), 128)],
            wpz_s.at[step], wpz_r.at[index], along_z(step),
        )

    wp_sends = lax.rem(z, 4) == kind
    wp_own = pltpu.make_async_copy(
        wp_in.at[wp_rows, :],
        wp.at[wp_rows, pl.ds(pl.multiple_of((kind * 4 + z // 4) * 128, 128), 128)],
        loc_sem.at[14],
    )

    @pl.when(wp_sends)
    def _():
        each(1, 16, lambda step: wpz(step, z // 4).start())
        wp_own.start()

    for i, ref in enumerate((q_loc, k_loc, v_loc)):
        loaded(i)
        for clip in range(2):
            cl1[clip, i * 64 : (i + 1) * 64, :] = ref[:, clip, :]
    swap1 = remote(cl1.at[other], xb1.at[core], xs.at[0], xr.at[0], sibling)
    swap1.start()
    keep1 = pltpu.make_async_copy(cl1.at[core], xb1.at[core], loc_sem.at[15])
    keep1.start()

    swap1.wait_recv()
    keep1.wait()
    zero_rows = jnp.zeros((8, 128), F32)
    turned = []
    for i in range(3):
        rows = jnp.concatenate(
            [xb1[0, i * 64 : (i + 1) * 64, :], xb1[1, i * 64 : (i + 1) * 64, :]], axis=0
        ).astype(F32)
        turned.append(jnp.transpose(rows))
    for head in range(16):
        head_send[head] = jnp.concatenate(
            [part[head * 40 : head * 40 + 40] for part in turned] + [zero_rows], axis=0
        ).astype(BF16)
    chip_lanes = pl.ds(pl.multiple_of(chip * 128, 128), 128)

    def qkv_copy(step):
        to = lax.rem(chip + step, 16)
        return remote(head_send.at[to], qkv.at[:, chip_lanes], qs.at[step], qr.at[step], on_chip(to))

    each(1, 16, lambda step: qkv_copy(step).start())
    qkv_own = pltpu.make_async_copy(head_send.at[chip], qkv.at[:, chip_lanes], loc_sem.at[18])
    qkv_own.start()

    for index in range(4):
        @pl.when(kind + 4 * index != z)
        def _():
            wpz(1, index).wait_recv()

    @pl.when(wp_sends)
    def _():
        wp_own.wait()

    def wp1(step):
        block = wp.at[wp_rows, pl.ds(pl.multiple_of(kind * 512, 128), 512)]
        return remote(block, block, wp1_s.at[step], wp1_r.at[step], along_a(step))

    for step in range(1, 4):
        wp1(step).start()

    group8 = a + 4 * core

    class Slab:
        def __init__(self, rows, held, full, sems, own_sem):
            self.rows, self.held, self.full = rows, held, full
            self.zs, self.zr, self.s1, self.r1, self.s2, self.r2, self.s3, self.r3 = sems
            self.part = pl.ds(pl.multiple_of(b * rows, 16), rows)
            self.sends = lax.rem(z, 8) == group8
            self.own = pltpu.make_async_copy(
                held.at[self.part, :], full.at[group8 * 2 + z // 8, self.part, :], own_sem
            )

        def deep(self, step, index):
            return remote(
                self.held.at[self.part, :], self.full.at[group8 * 2 + index, self.part, :],
                self.zs.at[step], self.zr.at[index], along_z(step),
            )

        def start_deep(self):
            @pl.when(self.sends)
            def _():
                each(1, 16, lambda step: self.deep(step, z // 8).start())
                self.own.start()

        def wait_deep(self):
            for index in range(2):
                @pl.when(group8 + 8 * index != z)
                def _():
                    self.deep(1, index).wait_recv()

            @pl.when(self.sends)
            def _():
                self.own.wait()

        def one(self, step):
            block = self.full.at[pl.ds(group8 * 2, 2), self.part, :]
            return remote(block, block, self.s1.at[step], self.r1.at[step], along_a(step))

        def band(self, number):
            return self.full.at[
                pl.ds(core * 8, 8), pl.ds(pl.multiple_of(number * self.rows, 16), self.rows), :
            ]

        def two(self, step):
            return remote(self.band(b), self.band(b), self.s2.at[step], self.r2.at[step], along_b(step))

        def cross(self, step):
            band = self.band(lax.rem(b - step + 4, 4))
            return remote(band, band, self.s3.at[step], self.r3.at[step], sibling)

        def sent(self):
            @pl.when(self.sends)
            def _():
                each(1, 16, lambda step: self.deep(step, z // 8).wait_send())

            for step in range(1, 4):
                self.one(step).wait_send()
                self.two(step).wait_send()
            for step in range(4):
                self.cross(step).wait_send()

    slab_a = Slab(
        16, a_slab, wa, (waz_s, waz_r, wa1_s, wa1_r, wa2_s, wa2_r, wac_s, wac_r), loc_sem.at[16]
    )
    slab_b = Slab(
        64, b_slab, wb, (wbz_s, wbz_r, wb1_s, wb1_r, wb2_s, wb2_r, wbc_s, wbc_r), loc_sem.at[17]
    )
    loaded(3)
    loaded(4)
    parts = [wo_loc[...].astype(F32)] + [wc1_loc[i].astype(F32) for i in range(3)]
    a_slab[...] = jnp.concatenate(parts, axis=0).astype(BF16)
    slab_a.start_deep()
    loaded(5)
    loaded(6)
    parts = [wqkv_loc[i].astype(F32) for i in range(3)] + [wc2_loc[i].astype(F32) for i in range(3)]
    b_slab[...] = jnp.concatenate(parts + [jnp.zeros((16, WIDTH), F32)], axis=0).astype(BF16)
    slab_b.start_deep()

    for step in range(1, 4):
        wp1(step).wait_recv()

    def wp_set(number):
        return wp.at[
            pl.ds(pl.multiple_of(number * 160, 16), 160), pl.ds(pl.multiple_of(core * 1024, 128), 1024)
        ]

    def wp2(step):
        return remote(wp_set(b), wp_set(b), wp2_s.at[step], wp2_r.at[step], along_b(step))

    def wpc(step):
        held = wp_set(lax.rem(b - step + 4, 4))
        return remote(held, held, wpc_s.at[step], wpc_r.at[step], sibling)

    for step in (2, 1, 3):
        wp2(step).start()
    wpc(0).start()

    for step in (1, 3, 2):
        wp2(step).wait_recv()
        wpc(step).start()

    slab_a.wait_deep()
    for step in range(1, 4):
        slab_a.one(step).start()
    slab_b.wait_deep()
    for step in range(1, 4):
        slab_b.one(step).start()

    loaded(9)
    for step in range(4):
        wpc(step).wait_recv()

    total = jnp.zeros((192, WIDTH), F32)
    for number in range(4):
        rows = jnp.concatenate(
            [g_loc[:, (number + 4 * i) * 128 : (number + 4 * i + 1) * 128] for i in range(4)], axis=1
        )
        total = total + dot(rows, wp[:, number * 512 : (number + 1) * 512], NT)
    slot_row = lax.broadcasted_iota(jnp.int32, (256, 192), 0)
    held_row = lax.broadcasted_iota(jnp.int32, (256, 192), 1)
    order = (lax.rem(slot_row, 16) * 16 + slot_row // 16 == held_row).astype(F32).astype(BF16)
    u_send[...] = dot(order, total.astype(BF16), NN).astype(BF16).reshape(16, 16, WIDTH)

    def u_copy(step):
        to = lax.rem(z + step, 16)
        return remote(u_send.at[to], u_recv.at[z], us.at[step], ur.at[step], (to, e))

    each(1, 16, lambda step: u_copy(step).start())
    u_own = pltpu.make_async_copy(u_send.at[z], u_recv.at[z], loc_sem.at[19])
    u_own.start()

    loaded(7)
    loaded(8)
    for clip in range(2):
        cl2[clip, 0:64, :] = c2_loc[:, clip, :]
        cl2[clip, 64:192, :] = c1_loc[:, clip, :]
    swap2 = remote(cl2.at[other], xb2.at[core], xs.at[1], xr.at[1], sibling)
    swap2.start()
    keep2 = pltpu.make_async_copy(cl2.at[core], xb2.at[core], loc_sem.at[20])
    keep2.start()

    for slab in (slab_a, slab_b):
        for step in range(1, 4):
            slab.one(step).wait_recv()
        for step in (2, 1, 3):
            slab.two(step).start()
        slab.cross(0).start()

    swap2.wait_recv()
    keep2.wait()
    after = on_chip(lax.rem(chip + 1, 16))
    before = on_chip(lax.rem(chip + 15, 16))
    edge_up = remote(xb2.at[1, pl.ds(176, 16), :], halo1.at[0], hs.at[0], hr.at[0], after)
    edge_down = remote(xb2.at[0, pl.ds(64, 16), :], halo1.at[1], hs.at[1], hr.at[1], before)
    edge_up.start()
    edge_down.start()

    each(1, 16, lambda step: qkv_copy(step).wait_recv())
    qkv_own.wait()
    row8 = lax.broadcasted_iota(jnp.int32, (8, LENGTH), 0)
    places = lax.broadcasted_iota(jnp.int32, (8, LENGTH), 1)
    own_count = jnp.where(core == 0, counts[0, 0], counts[0, 1])
    ones_rows = jnp.where(row8 == 0, 1.0, 0.0)
    bias_rows = jnp.where((row8 == 0) & (places >= own_count), MASKED, 0.0)
    arrived = qkv[...].astype(F32)
    wide_q = jnp.concatenate([arrived[0:40], ones_rows], axis=0)
    wide_k = jnp.concatenate([arrived[40:80], bias_rows], axis=0)
    wide_v = arrived[80:128]
    qt[...] = wide_q.astype(BF16)
    kt[...] = wide_k.astype(BF16)
    vt[...] = wide_v.astype(BF16)
    qn[...] = jnp.transpose(wide_q).astype(BF16)
    kn[...] = jnp.transpose(wide_k).astype(BF16)
    vn[...] = jnp.transpose(wide_v).astype(BF16)

    def exponentials(number):
        lanes = pl.ds(pl.multiple_of(number * QB, QB), QB)
        big[...] = dot(kn[...], qt[:, lanes], NN)
        highest = jnp.max(big[...], axis=0, keepdims=True)
        weights = jnp.exp2((big[...] - highest) * (SCALE * LOG2E))
        weights_b = weights.astype(BF16)
        e_mat[:, lanes] = weights_b
        share = 1.0 / jnp.sum(weights, axis=0, keepdims=True)
        rl[:, lanes] = share
        attn[:, lanes] = dot(vt[...], weights_b, NN) * share

    each(0, LENGTH // QB, exponentials)

    for step in (1, 3, 2):
        slab_a.two(step).wait_recv()
        slab_a.cross(step).start()
    for step in range(4):
        slab_a.cross(step).wait_recv()

    def slabs_of(full, number):
        return [full[lax.rem(place, 8) * 2 + place // 8].astype(F32) for place in (2 * number, 2 * number + 1)]

    def compact_a(number):
        slabs = slabs_of(wa, number)
        rows = pl.ds(pl.multiple_of(number * 80, 16), 80)
        w_full[0, rows, :] = jnp.concatenate([slab[0:40] for slab in slabs], axis=0).astype(BF16)
        for i in range(3):
            w_last[pl.ds(pl.multiple_of(i * 128 + number * 16, 16), 16), :] = jnp.concatenate(
                [slab[40 + i * 8 : 48 + i * 8] for slab in slabs], axis=0
            ).astype(BF16)

    each(0, 8, compact_a)

    loaded(11)
    slots = lax.broadcasted_iota(jnp.int32, (256, 64), 0)
    frame = e * 64 + lax.broadcasted_iota(jnp.int32, (256, 64), 1)
    named = []
    for clip in range(2):
        hit = (target[clip : clip + 1, :] == slots // 16) & (frame < counts[0, clip])
        named.append(jnp.where(hit, 1.0, 0.0))
    earlier = lax.broadcasted_iota(jnp.int32, (64, 64), 0)
    later = lax.broadcasted_iota(jnp.int32, (64, 64), 1)
    upto = (earlier <= later).astype(F32).astype(BF16)
    under = (earlier < later).astype(F32).astype(BF16)
    named_b = [part.astype(BF16) for part in named]
    seen = [
        dot(named_b[0], upto, NN) + dot(named_b[1], under, NN),
        dot(named_b[0], upto, NN) + dot(named_b[1], upto, NN),
    ]
    within = lax.rem(slots, 16).astype(F32) + 1.0
    choose = jnp.transpose(
        jnp.concatenate([jnp.where(seen[i] == within, named[i], 0.0) for i in range(2)], axis=1)
    ).astype(BF16)

    each(1, 16, lambda step: u_copy(step).wait_recv())
    u_own.wait()
    up_send[...] = (
        dot(choose, u_recv[...].reshape(256, WIDTH), NN).astype(BF16).reshape(2, 64, WIDTH)
    )
    swap3 = remote(up_send.at[other], up.at[core], xs.at[2], xr.at[2], sibling)
    swap3.start()
    keep3 = pltpu.make_async_copy(up_send.at[core], up.at[core], loc_sem.at[21])
    keep3.start()
    swap3.wait_recv()
    keep3.wait()
    d_attn = dot(w_full[0], up[...].reshape(128, WIDTH), NT)
    for head in range(16):
        d_send[head] = jnp.concatenate([d_attn[head * 40 : head * 40 + 40], zero_rows], axis=0).astype(
            BF16
        )

    def d_copy(step):
        to = lax.rem(chip + step, 16)
        return remote(d_send.at[to], d_out.at[:, chip_lanes], ds_.at[step], dr.at[step], on_chip(to))

    each(1, 16, lambda step: d_copy(step).start())
    d_own = pltpu.make_async_copy(d_send.at[chip], d_out.at[:, chip_lanes], loc_sem.at[22])
    d_own.start()

    edge_up.wait_recv()
    edge_down.wait_recv()
    for i in range(5):
        lanes = slice(i * 128, i * 128 + 128)
        slope1[i, 0:16, :] = gelu_slope(halo1[0, :, lanes].astype(F32))
        slope1[i, 16:144, :] = gelu_slope(xb2[0, 64:192, lanes].astype(F32))
        slope1[i, 144:272, :] = gelu_slope(xb2[1, 64:192, lanes].astype(F32))
        slope1[i, 272:288, :] = gelu_slope(halo1[1, :, lanes].astype(F32))

    each(1, 16, lambda step: d_copy(step).wait_recv())
    d_own.wait()
    shared = d_out[...].astype(F32) * rl[...]
    d_out[...] = shared.astype(BF16)
    dn[...] = jnp.transpose(shared).astype(BF16)
    delta[...] = jnp.sum(shared * attn[...], axis=0, keepdims=True)
    dk_acc[...] = jnp.zeros_like(dk_acc)
    dv_acc[...] = jnp.zeros_like(dv_acc)

    def place_lanes(ref, number):
        return ref.at[:, pl.ds(pl.multiple_of(number * 128, 128), 128)]

    def b_copy(step):
        to = lax.rem(chip + step, 16)
        return remote(place_lanes(dq_t, to), dq_recv.at[chip], bs.at[step], br.at[step], on_chip(to))

    def gradients(number):
        block = lax.rem(chip // (QB // 128) + number, LENGTH // QB)
        lanes = pl.ds(pl.multiple_of(block * QB, QB), QB)
        weights = e_mat[:, lanes]
        moved = dot(vn[...], d_out[:, lanes], NN) - delta[:, lanes]
        slopes = (weights.astype(F32) * moved).astype(BF16)
        dq_t[:, lanes] = (dot(kt[...], slopes, NN) * SCALE).astype(BF16)
        for part in range(QB // 128):
            step = lax.rem(QB // 128 * block + part - chip + 16, 16)

            @pl.when(step > 0)
            def _():
                b_copy(step).start()

        dv_acc[...] += dot(weights, dn[lanes, :], NN)
        dk_acc[...] += dot(slopes, qn[lanes, :], NN)

    each(0, LENGTH // QB, gradients)
    turned = jnp.transpose(dk_acc[...] * SCALE)[0:40]
    dkv_t[...] = jnp.concatenate([turned, jnp.transpose(dv_acc[...])[0:40]], axis=0).astype(BF16)

    def c_copy(step):
        to = lax.rem(chip + step, 16)
        return remote(place_lanes(dkv_t, to), dkv_recv.at[chip], cs.at[step], cr.at[step], on_chip(to))

    each(1, 16, lambda step: c_copy(step).start())
    b_own = pltpu.make_async_copy(place_lanes(dq_t, chip), dq_recv.at[chip], loc_sem.at[23])
    c_own = pltpu.make_async_copy(place_lanes(dkv_t, chip), dkv_recv.at[chip], loc_sem.at[24])
    b_own.start()
    c_own.start()

    for step in (1, 3, 2):
        slab_b.two(step).wait_recv()
        slab_b.cross(step).start()

    loaded(10)
    loaded(12)
    loaded(13)
    pre_two = jnp.concatenate([xb2[0, 0:64, :], xb2[1, 0:64, :]], axis=0).astype(F32)
    slope2 = gelu_slope(pre_two)
    layer_in = gelu_value(pre_two) + pair[0:1] * near[0] + pair[1:2] * near[1]
    center = jnp.mean(layer_in, axis=-1, keepdims=True)
    moved = layer_in - center
    rstd = 1.0 / jnp.sqrt(jnp.mean(moved * moved, axis=-1, keepdims=True) + 1e-05)
    normed = moved * rstd

    for step in range(4):
        slab_b.cross(step).wait_recv()

    def compact_b(number):
        slabs = slabs_of(wb, number)
        rows = pl.ds(pl.multiple_of(number * 80, 16), 80)
        for i in range(6):
            w_full[1 + i, rows, :] = jnp.concatenate(
                [slab[i * 40 : i * 40 + 40] for slab in slabs], axis=0
            ).astype(BF16)

    each(0, 8, compact_b)

    @pl.when(wp_sends)
    def _():
        each(1, 16, lambda step: wpz(step, z // 4).wait_send())

    for step in range(1, 4):
        for copy in (wp1, wp2, wpc):
            copy(step).wait_send()
    wpc(0).wait_send()
    slab_a.sent()
    slab_b.sent()

    def sent(step):
        for copy in (qkv_copy, u_copy, d_copy, b_copy):
            copy(step).wait_send()

    each(1, 16, sent)
    for copy in (swap1, swap2, swap3, edge_up, edge_down):
        copy.wait_send()

    each(1, 16, lambda step: b_copy(step).wait_recv())
    b_own.wait()
    c_own.wait()
    each(1, 16, lambda step: c_copy(step).wait_recv())
    d_normed = jnp.zeros((128, WIDTH), F32)
    for i, (ref, low) in enumerate(((dq_recv, 0), (dkv_recv, 0), (dkv_recv, 40))):
        turned = jnp.concatenate([ref[head].astype(F32)[low : low + 40] for head in range(16)], axis=0)
        d_normed = d_normed + dot(jnp.transpose(turned).astype(BF16), w_full[1 + i], NT)
    scaled = d_normed * gain[...].reshape(1, WIDTH)
    d_layer = rstd * (
        scaled
        - jnp.mean(scaled, axis=-1, keepdims=True)
        - normed * jnp.mean(scaled * normed, axis=-1, keepdims=True)
    )
    d2_buf[...] = ((up[...].reshape(128, WIDTH).astype(F32) + d_layer) * slope2).astype(BF16)
    row_up = remote(d2_buf.at[pl.ds(112, 16), :], halo2.at[0], hs.at[2], hr.at[2], after)
    row_down = remote(d2_buf.at[pl.ds(0, 16), :], halo2.at[1], hs.at[3], hr.at[3], before)
    row_up.start()
    row_down.start()
    each(1, 16, lambda step: c_copy(step).wait_send())
    row_up.wait_recv()
    row_down.wait_recv()
    has_before = jnp.where(chip > 0, 1.0, 0.0).astype(BF16)
    has_after = jnp.where(chip < 15, 1.0, 0.0).astype(BF16)
    rows = jnp.concatenate([halo2[0] * has_before, d2_buf[...], halo2[1] * has_after], axis=0)
    tap0, tap1, tap2 = (dot(rows, w_full[4 + i], NT) for i in range(3))
    even_slope = jnp.concatenate([slope1[i, pl.ds(16, 136, stride=2), :] for i in range(5)], axis=1)
    odd_slope = jnp.concatenate([slope1[i, pl.ds(1, 136, stride=2), :] for i in range(5)], axis=1)
    spot = lax.broadcasted_iota(jnp.int32, (136, 1), 0)
    even = tap1[16:152] * even_slope
    even = jnp.where((spot < 128) | (chip < 15), even, 0.0).astype(BF16)
    odd = (tap2[8:144] + tap0[9:145]) * odd_slope
    odd = jnp.where((spot >= 8) | (chip > 0), odd, 0.0).astype(BF16)
    even_mel = dot(even, w_last[...], NT)
    odd_mel = dot(odd, w_last[...], NT)
    mel_even = odd_mel[8:136, 0:128] + even_mel[0:128, 128:256] + odd_mel[7:135, 256:384]
    mel_odd = even_mel[1:129, 0:128] + odd_mel[8:136, 128:256] + even_mel[0:128, 256:384]
    for block in range(2):
        mel_buf[block, 0:64, :] = mel_even[block * 64 : block * 64 + 64]
        mel_buf[block, 64:128, :] = mel_odd[block * 64 : block * 64 + 64]
    swap4 = remote(mel_buf.at[other], mel_recv, xs.at[3], xr.at[3], sibling)
    swap4.start()
    for half in range(2):
        own = mel_buf[core, half * 64 : half * 64 + 64, :]
        out[pl.ds(2 * half + core, 64, stride=4), :] = own
    swap4.wait_recv()
    for half in range(2):
        out[pl.ds(2 * half + other, 64, stride=4), :] = mel_recv[half * 64 : half * 64 + 64, :]
    for copy in (swap4, row_up, row_down):
        copy.wait_send()


def per_device(
    frame_counts, dest_rank, grad_rows, queries, key_rows, value_rows, conv2_pre, conv1_pre,
    norm_gain, w_proj, w_out, w_qkv, w_conv2, w_conv1,
):
    chip_tab, near_tab = tables()
    target = jnp.transpose(dest_rank[0, :, :, 0])
    grads = jnp.transpose(grad_rows[0], (1, 0, 2)).reshape(192, HID)
    anywhere = pl.BlockSpec(memory_space=pl.ANY)
    vmem = pl.BlockSpec(memory_space=pltpu.VMEM)
    scratch = [
        ((2, 64), jnp.int32), ((WIDTH,), F32), ((2, WIDTH), F32),
        ((192, HID), BF16), ((64, 2, WIDTH), BF16), ((64, 2, WIDTH), BF16), ((64, 2, WIDTH), BF16),
        ((64, 2, WIDTH), BF16), ((128, 2, WIDTH), BF16), ((40, WIDTH), BF16), ((3, 40, WIDTH), BF16),
        ((3, 40, WIDTH), BF16), ((3, 8, WIDTH), BF16), ((2, 128, WIDTH), F32),
        ((64, WIDTH), BF16), ((256, WIDTH), BF16), ((WIDTH, HID), BF16), ((16, 64, WIDTH), BF16),
        ((16, 256, WIDTH), BF16), ((7, WIDTH, WIDTH), BF16), ((384, WIDTH), BF16),
        ((2, 192, WIDTH), BF16), ((2, 192, WIDTH), BF16), ((2, 192, WIDTH), BF16), ((2, 192, WIDTH), BF16),
        ((16, 128, 128), BF16), ((128, LENGTH), BF16), ((48, LENGTH), BF16), ((48, LENGTH), BF16), ((48, LENGTH), BF16),
        ((LENGTH, 48), BF16), ((LENGTH, 48), BF16), ((LENGTH, 48), BF16),
        ((16, 16, WIDTH), BF16), ((16, 16, WIDTH), BF16), ((2, 64, WIDTH), BF16), ((2, 64, WIDTH), BF16),
        ((16, 48, 128), BF16), ((48, LENGTH), BF16), ((LENGTH, 48), BF16),
        ((LENGTH, LENGTH), BF16), ((LENGTH, QB), F32), ((1, LENGTH), F32), ((1, LENGTH), F32), ((48, LENGTH), F32), ((LENGTH, 48), F32),
        ((LENGTH, 48), F32), ((48, LENGTH), BF16), ((80, LENGTH), BF16), ((16, 48, 128), BF16),
        ((16, 80, 128), BF16),
        ((5, 288, 128), F32), ((2, 16, WIDTH), BF16), ((128, WIDTH), BF16), ((2, 16, WIDTH), BF16),
        ((2, 128, 128), F32), ((128, 128), F32),
    ]
    sems = [25, 16] + [4] * 7 + [16, 2] + [4] * 6 + [16, 2] + [4] * 6 + [4, 4] + [16] * 10 + [4, 4]
    result = pl.pallas_call(
        kernel,
        out_shape=jax.ShapeDtypeStruct((256, 128), F32),
        in_specs=[pl.BlockSpec(memory_space=pltpu.SMEM)] + [anywhere] * 15,
        out_specs=vmem,
        scratch_shapes=[pltpu.VMEM(shape, kind) for shape, kind in scratch]
        + [pltpu.SemaphoreType.DMA((n,)) for n in sems],
        compiler_params=pltpu.CompilerParams(
            collective_id=0, has_side_effects=True, vmem_limit_bytes=58 << 20
        ),
    )(
        frame_counts, target, grads, queries, key_rows, value_rows, conv2_pre, conv1_pre,
        norm_gain, w_proj, w_out, w_qkv, w_conv2, w_conv1,
        jnp.asarray(chip_tab), jnp.asarray(near_tab),
    )
    return result.reshape(1, 128, 2, 128)


def solution(mesh):
    rows = P("llm", "enc", None, None)
    placed = (
        P("llm", None), rows, P("llm", None, "enc", None), rows, rows, rows, rows, rows, P(),
        P(None, "llm"), P("llm", None), P(None, "llm", None), P(None, "llm", None), P(None, "llm", None),
    )
    return jax.shard_map(
        per_device, mesh=mesh, in_specs=placed, out_specs=rows, check_vma=False
    )
```

```python
import functools

import jax
import jax.numpy as jnp
import numpy as np
from jax import lax
from jax.experimental import pallas as pl
from jax.experimental.pallas import tpu as pltpu
from jax.sharding import PartitionSpec as P

MESH = pl.DeviceIdType.MESH
F32, BF16 = jnp.float32, jnp.bfloat16
HEAD_DIM = 40
WIDTH = 640
HID = 2048
LENGTH = 2048
SCALE = HEAD_DIM ** (-0.5)
LOG2E = 1.4426950408889634
MASKED = -1e30
ROOT_HALF = 0.7071067811865476
INV_ROOT_TWO_PI = 0.3989422804014327
QB = 512


def gelu_value(value):
    return value * 0.5 * (1.0 + lax.erf(value * ROOT_HALF))


def gelu_slope(value):
    return (
        0.5 * (1.0 + lax.erf(value * ROOT_HALF))
        + value * jnp.exp(-0.5 * value * value) * INV_ROOT_TWO_PI
    )


def dot(a, b, dims):
    return lax.dot_general(a, b, (dims, ((), ())), preferred_element_type=F32)


NN = ((1,), (0,))
NT = ((1,), (1,))
TN = ((0,), (0,))


def tables():
    inverse = 10000.0 ** (-np.arange(320) / 319.0)
    base = 128.0 * np.arange(16)[:, None] * inverse[None, :]
    local = np.arange(128.0)[:, None] * inverse[None, :]
    first = np.concatenate([np.sin(base), np.cos(base)], axis=1)
    second = np.concatenate([np.cos(base), -np.sin(base)], axis=1)
    chip = np.stack([first, second], axis=1).astype(np.float32)
    near = np.stack(
        [np.concatenate([np.cos(local)] * 2, 1), np.concatenate([np.sin(local)] * 2, 1)]
    ).astype(np.float32)
    return chip, near


def kernel(
    counts, target_in, grads, q_in, k_in, v_in, c2_in, c1_in, gain_in, wp_in, wo_in, wqkv_in, wc2_in, wc1_in,
    chip_tab, near_tab,
    out,
    target, gain, pair, g_loc, q_loc, k_loc, v_loc, c2_loc, c1_loc, wo_loc, wqkv_loc, wc2_loc, wc1_loc, near,
    a_slab, b_slab, wp, wa, wb, w_full, w_last,
    cl1, cl2, xb1, xb2, head_send, qkv, qt, kt, vt, kn, vn, qn,
    u_send, u_recv, up_send, up, d_send, d_out, dn,
    e_mat, big, rl, delta, attn, dk_acc, dq_t, dk_t, dv_t, dq_recv, dk_recv, dv_recv,
    slope1, halo1, d2_buf, halo2, mel_buf, mel_recv,
    loc_sem, wpz_s, wpz_r, wp1_s, wp1_r, wp2_s, wp2_r, wpc_s, wpc_r,
    waz_s, waz_r, wa1_s, wa1_r, wa2_s, wa2_r, wac_s, wac_r,
    wbz_s, wbz_r, wb1_s, wb1_r, wb2_s, wb2_r, wbc_s, wbc_r,
    xs, xr, qs, qr, us, ur, ds_, dr, bs, br, cs, cr, vs, vr, hs, hr,
):
    z = lax.axis_index("llm")
    e = lax.axis_index("enc")
    core = lax.rem(e, 2)
    other = 1 - core
    chip = e // 2
    x = lax.rem(chip, 4)
    y = chip // 4
    a = jnp.where(core == 0, x, y)
    b = jnp.where(core == 0, y, x)
    sibling = (z, chip * 2 + other)

    def along_a(step):
        to = lax.rem(a + step, 4)
        return (z, jnp.where(core == 0, y * 4 + to, to * 4 + x) * 2 + core)

    def along_b(step):
        to = lax.rem(b + step, 4)
        return (z, jnp.where(core == 0, to * 4 + x, y * 4 + to) * 2 + core)

    def along_z(step):
        return (lax.rem(z + step, 16), e)

    def on_chip(number):
        return (z, number * 2 + core)

    def remote(src, dst, send, recv, device):
        return pltpu.make_async_remote_copy(
            src_ref=src, dst_ref=dst, send_sem=send, recv_sem=recv, device_id=device, device_id_type=MESH
        )

    def each(low, high, act):
        def body(step, carry):
            act(step)
            return carry

        lax.fori_loop(low, high, body, 0)

    barrier = pltpu.get_barrier_semaphore()

    def greet(step):
        pl.semaphore_signal(barrier, inc=1, device_id=along_z(step), device_id_type=MESH)
        pl.semaphore_signal(
            barrier, inc=1, device_id=on_chip(lax.rem(chip + step, 16)), device_id_type=MESH
        )

    each(1, 16, greet)
    pl.semaphore_signal(barrier, inc=1, device_id=sibling, device_id_type=MESH)

    loads = [
        (q_in.at[0], q_loc), (k_in.at[0], k_loc), (v_in.at[0], v_loc), (wo_in, wo_loc), (wc1_in, wc1_loc),
        (wqkv_in, wqkv_loc), (wc2_in, wc2_loc), (c2_in.at[0], c2_loc), (c1_in.at[0], c1_loc),
        (grads, g_loc), (near_tab, near), (target_in, target), (gain_in, gain), (chip_tab.at[chip], pair),
    ]
    for i, (src, dst) in enumerate(loads):
        pltpu.make_async_copy(src, dst, loc_sem.at[i]).start()

    def loaded(i):
        pltpu.make_async_copy(loads[i][0], loads[i][1], loc_sem.at[i]).wait()

    pl.semaphore_wait(barrier, 31)

    piece = 2 * b + a // 2
    kind = lax.rem(a, 2) + 2 * core
    wp_rows = pl.ds(pl.multiple_of(piece * 80, 16), 80)

    def wpz(step, index):
        return remote(
            wp_in.at[wp_rows, :],
            wp.at[wp_rows, pl.ds(pl.multiple_of((kind * 4 + index) * 128, 128), 128)],
            wpz_s.at[step], wpz_r.at[index], along_z(step),
        )

    wp_sends = lax.rem(z, 4) == kind
    wp_own = pltpu.make_async_copy(
        wp_in.at[wp_rows, :],
        wp.at[wp_rows, pl.ds(pl.multiple_of((kind * 4 + z // 4) * 128, 128), 128)],
        loc_sem.at[14],
    )

    @pl.when(wp_sends)
    def _():
        each(1, 16, lambda step: wpz(step, z // 4).start())
        wp_own.start()

    for i, ref in enumerate((q_loc, k_loc, v_loc)):
        loaded(i)
        for clip in range(2):
            cl1[clip, i * 64 : (i + 1) * 64, :] = ref[:, clip, :]
    swap1 = remote(cl1.at[other], xb1.at[core], xs.at[0], xr.at[0], sibling)
    swap1.start()
    keep1 = pltpu.make_async_copy(cl1.at[core], xb1.at[core], loc_sem.at[15])
    keep1.start()

    swap1.wait_recv()
    keep1.wait()
    zero_rows = jnp.zeros((8, 128), F32)
    turned = []
    for i in range(3):
        rows = jnp.concatenate(
            [xb1[0, i * 64 : (i + 1) * 64, :], xb1[1, i * 64 : (i + 1) * 64, :]], axis=0
        ).astype(F32)
        turned.append(jnp.transpose(rows))
    for head in range(16):
        head_send[head] = jnp.concatenate(
            [part[head * 40 : head * 40 + 40] for part in turned] + [zero_rows], axis=0
        ).astype(BF16)
    chip_lanes = pl.ds(pl.multiple_of(chip * 128, 128), 128)

    def qkv_copy(step):
        to = lax.rem(chip + step, 16)
        return remote(head_send.at[to], qkv.at[:, chip_lanes], qs.at[step], qr.at[step], on_chip(to))

    each(1, 16, lambda step: qkv_copy(step).start())
    qkv_own = pltpu.make_async_copy(head_send.at[chip], qkv.at[:, chip_lanes], loc_sem.at[18])
    qkv_own.start()

    for index in range(4):
        @pl.when(kind + 4 * index != z)
        def _():
            wpz(1, index).wait_recv()

    @pl.when(wp_sends)
    def _():
        wp_own.wait()

    def wp1(step):
        block = wp.at[wp_rows, pl.ds(pl.multiple_of(kind * 512, 128), 512)]
        return remote(block, block, wp1_s.at[step], wp1_r.at[step], along_a(step))

    for step in range(1, 4):
        wp1(step).start()

    group8 = a + 4 * core

    class Slab:
        def __init__(self, rows, held, full, sems, own_sem):
            self.rows, self.held, self.full = rows, held, full
            self.zs, self.zr, self.s1, self.r1, self.s2, self.r2, self.s3, self.r3 = sems
            self.part = pl.ds(pl.multiple_of(b * rows, 16), rows)
            self.sends = lax.rem(z, 8) == group8
            self.own = pltpu.make_async_copy(
                held.at[self.part, :], full.at[group8 * 2 + z // 8, self.part, :], own_sem
            )

        def deep(self, step, index):
            return remote(
                self.held.at[self.part, :], self.full.at[group8 * 2 + index, self.part, :],
                self.zs.at[step], self.zr.at[index], along_z(step),
            )

        def start_deep(self):
            @pl.when(self.sends)
            def _():
                each(1, 16, lambda step: self.deep(step, z // 8).start())
                self.own.start()

        def wait_deep(self):
            for index in range(2):
                @pl.when(group8 + 8 * index != z)
                def _():
                    self.deep(1, index).wait_recv()

            @pl.when(self.sends)
            def _():
                self.own.wait()

        def one(self, step):
            block = self.full.at[pl.ds(group8 * 2, 2), self.part, :]
            return remote(block, block, self.s1.at[step], self.r1.at[step], along_a(step))

        def band(self, number):
            return self.full.at[
                pl.ds(core * 8, 8), pl.ds(pl.multiple_of(number * self.rows, 16), self.rows), :
            ]

        def two(self, step):
            return remote(self.band(b), self.band(b), self.s2.at[step], self.r2.at[step], along_b(step))

        def cross(self, step):
            band = self.band(lax.rem(b - step + 4, 4))
            return remote(band, band, self.s3.at[step], self.r3.at[step], sibling)

        def sent(self):
            @pl.when(self.sends)
            def _():
                each(1, 16, lambda step: self.deep(step, z // 8).wait_send())

            for step in range(1, 4):
                self.one(step).wait_send()
                self.two(step).wait_send()
            for step in range(4):
                self.cross(step).wait_send()

    slab_a = Slab(
        16, a_slab, wa, (waz_s, waz_r, wa1_s, wa1_r, wa2_s, wa2_r, wac_s, wac_r), loc_sem.at[16]
    )
    slab_b = Slab(
        64, b_slab, wb, (wbz_s, wbz_r, wb1_s, wb1_r, wb2_s, wb2_r, wbc_s, wbc_r), loc_sem.at[17]
    )
    loaded(3)
    loaded(4)
    parts = [wo_loc[...].astype(F32)] + [wc1_loc[i].astype(F32) for i in range(3)]
    a_slab[...] = jnp.concatenate(parts, axis=0).astype(BF16)
    slab_a.start_deep()
    loaded(5)
    loaded(6)
    parts = [wqkv_loc[i].astype(F32) for i in range(3)] + [wc2_loc[i].astype(F32) for i in range(3)]
    b_slab[...] = jnp.concatenate(parts + [jnp.zeros((16, WIDTH), F32)], axis=0).astype(BF16)
    slab_b.start_deep()

    for step in range(1, 4):
        wp1(step).wait_recv()

    def wp_set(number):
        return wp.at[
            pl.ds(pl.multiple_of(number * 160, 16), 160), pl.ds(pl.multiple_of(core * 1024, 128), 1024)
        ]

    def wp2(step):
        return remote(wp_set(b), wp_set(b), wp2_s.at[step], wp2_r.at[step], along_b(step))

    def wpc(step):
        held = wp_set(lax.rem(b - step + 4, 4))
        return remote(held, held, wpc_s.at[step], wpc_r.at[step], sibling)

    for step in (2, 1, 3):
        wp2(step).start()
    wpc(0).start()

    for step in (1, 3, 2):
        wp2(step).wait_recv()
        wpc(step).start()

    slab_a.wait_deep()
    for step in range(1, 4):
        slab_a.one(step).start()

    loaded(9)
    for step in range(4):
        wpc(step).wait_recv()

    total = jnp.zeros((192, WIDTH), F32)
    for number in range(4):
        rows = jnp.concatenate(
            [g_loc[:, (number + 4 * i) * 128 : (number + 4 * i + 1) * 128] for i in range(4)], axis=1
        )
        total = total + dot(rows, wp[:, number * 512 : (number + 1) * 512], NT)
    slot_row = lax.broadcasted_iota(jnp.int32, (256, 192), 0)
    held_row = lax.broadcasted_iota(jnp.int32, (256, 192), 1)
    order = (lax.rem(slot_row, 16) * 16 + slot_row // 16 == held_row).astype(F32).astype(BF16)
    u_send[...] = dot(order, total.astype(BF16), NN).astype(BF16).reshape(16, 16, WIDTH)

    def u_copy(step):
        to = lax.rem(z + step, 16)
        return remote(u_send.at[to], u_recv.at[z], us.at[step], ur.at[step], (to, e))

    each(1, 16, lambda step: u_copy(step).start())
    u_own = pltpu.make_async_copy(u_send.at[z], u_recv.at[z], loc_sem.at[19])
    u_own.start()

    loaded(7)
    loaded(8)
    for clip in range(2):
        cl2[clip, 0:64, :] = c2_loc[:, clip, :]
        cl2[clip, 64:192, :] = c1_loc[:, clip, :]
    swap2 = remote(cl2.at[other], xb2.at[core], xs.at[1], xr.at[1], sibling)
    swap2.start()
    keep2 = pltpu.make_async_copy(cl2.at[core], xb2.at[core], loc_sem.at[20])
    keep2.start()

    for step in range(1, 4):
        slab_a.one(step).wait_recv()
    for step in (2, 1, 3):
        slab_a.two(step).start()
    slab_a.cross(0).start()
    slab_b.wait_deep()
    for step in range(1, 4):
        slab_b.one(step).start()

    swap2.wait_recv()
    keep2.wait()
    after = on_chip(lax.rem(chip + 1, 16))
    before = on_chip(lax.rem(chip + 15, 16))
    edge_up = remote(xb2.at[1, pl.ds(176, 16), :], halo1.at[0], hs.at[0], hr.at[0], after)
    edge_down = remote(xb2.at[0, pl.ds(64, 16), :], halo1.at[1], hs.at[1], hr.at[1], before)
    edge_up.start()
    edge_down.start()

    each(1, 16, lambda step: qkv_copy(step).wait_recv())
    qkv_own.wait()
    row8 = lax.broadcasted_iota(jnp.int32, (8, LENGTH), 0)
    places = lax.broadcasted_iota(jnp.int32, (8, LENGTH), 1)
    own_count = jnp.where(core == 0, counts[0, 0], counts[0, 1])
    ones_rows = jnp.where(row8 == 0, 1.0, 0.0)
    bias_rows = jnp.where((row8 == 0) & (places >= own_count), MASKED, 0.0)
    arrived = qkv[...].astype(F32)
    wide_q = jnp.concatenate([arrived[0:40], ones_rows], axis=0)
    wide_k = jnp.concatenate([arrived[40:80], bias_rows], axis=0)
    wide_v = arrived[80:128]
    qt[...] = wide_q.astype(BF16)
    kt[...] = wide_k.astype(BF16)
    vt[...] = wide_v.astype(BF16)
    qn[...] = jnp.transpose(wide_q).astype(BF16)
    kn[...] = jnp.transpose(wide_k).astype(BF16)
    vn[...] = jnp.transpose(wide_v).astype(BF16)

    def exponentials(number):
        lanes = pl.ds(pl.multiple_of(number * QB, QB), QB)
        big[...] = dot(kn[...], qt[:, lanes], NN)
        highest = jnp.max(big[...], axis=0, keepdims=True)
        weights = jnp.exp2((big[...] - highest) * (SCALE * LOG2E))
        weights_b = weights.astype(BF16)
        e_mat[:, lanes] = weights_b
        share = 1.0 / jnp.sum(weights, axis=0, keepdims=True)
        rl[:, lanes] = share
        attn[:, lanes] = dot(vt[...], weights_b, NN) * share

    each(0, LENGTH // QB, exponentials)

    for step in (1, 3, 2):
        slab_a.two(step).wait_recv()
        slab_a.cross(step).start()
    for step in range(1, 4):
        slab_b.one(step).wait_recv()
    for step in (2, 1, 3):
        slab_b.two(step).start()
    slab_b.cross(0).start()
    for step in range(4):
        slab_a.cross(step).wait_recv()

    def slabs_of(full, number):
        return [full[lax.rem(place, 8) * 2 + place // 8].astype(F32) for place in (2 * number, 2 * number + 1)]

    def compact_a(number):
        slabs = slabs_of(wa, number)
        rows = pl.ds(pl.multiple_of(number * 80, 16), 80)
        w_full[0, rows, :] = jnp.concatenate([slab[0:40] for slab in slabs], axis=0).astype(BF16)
        for i in range(3):
            w_last[pl.ds(pl.multiple_of(i * 128 + number * 16, 16), 16), :] = jnp.concatenate(
                [slab[40 + i * 8 : 48 + i * 8] for slab in slabs], axis=0
            ).astype(BF16)

    each(0, 8, compact_a)

    loaded(11)
    slots = lax.broadcasted_iota(jnp.int32, (256, 64), 0)
    frame = e * 64 + lax.broadcasted_iota(jnp.int32, (256, 64), 1)
    named = []
    for clip in range(2):
        hit = (target[clip : clip + 1, :] == slots // 16) & (frame < counts[0, clip])
        named.append(jnp.where(hit, 1.0, 0.0))
    earlier = lax.broadcasted_iota(jnp.int32, (64, 64), 0)
    later = lax.broadcasted_iota(jnp.int32, (64, 64), 1)
    upto = (earlier <= later).astype(F32).astype(BF16)
    under = (earlier < later).astype(F32).astype(BF16)
    named_b = [part.astype(BF16) for part in named]
    seen = [
        dot(named_b[0], upto, NN) + dot(named_b[1], under, NN),
        dot(named_b[0], upto, NN) + dot(named_b[1], upto, NN),
    ]
    within = lax.rem(slots, 16).astype(F32) + 1.0
    choose = jnp.transpose(
        jnp.concatenate([jnp.where(seen[i] == within, named[i], 0.0) for i in range(2)], axis=1)
    ).astype(BF16)

    @pl.when(wp_sends)
    def _():
        each(1, 16, lambda step: wpz(step, z // 4).wait_send())

    for step in range(1, 4):
        for copy in (wp1, wp2, wpc):
            copy(step).wait_send()
    wpc(0).wait_send()
    slab_a.sent()
    each(1, 16, lambda step: qkv_copy(step).wait_send())

    each(1, 16, lambda step: u_copy(step).wait_recv())
    u_own.wait()
    up_send[...] = (
        dot(choose, u_recv[...].reshape(256, WIDTH), NN).astype(BF16).reshape(2, 64, WIDTH)
    )
    swap3 = remote(up_send.at[other], up.at[core], xs.at[2], xr.at[2], sibling)
    swap3.start()
    keep3 = pltpu.make_async_copy(up_send.at[core], up.at[core], loc_sem.at[21])
    keep3.start()
    swap3.wait_recv()
    keep3.wait()
    d_attn = dot(w_full[0], up[...].reshape(128, WIDTH), NT)
    for head in range(16):
        d_send[head] = jnp.concatenate([d_attn[head * 40 : head * 40 + 40], zero_rows], axis=0).astype(
            BF16
        )

    def d_copy(step):
        to = lax.rem(chip + step, 16)
        return remote(d_send.at[to], d_out.at[:, chip_lanes], ds_.at[step], dr.at[step], on_chip(to))

    each(1, 16, lambda step: d_copy(step).start())
    d_own = pltpu.make_async_copy(d_send.at[chip], d_out.at[:, chip_lanes], loc_sem.at[22])
    d_own.start()

    edge_up.wait_recv()
    edge_down.wait_recv()
    for i in range(5):
        lanes = slice(i * 128, i * 128 + 128)
        slope1[i, 0:16, :] = gelu_slope(halo1[0, :, lanes].astype(F32))
        slope1[i, 16:144, :] = gelu_slope(xb2[0, 64:192, lanes].astype(F32))
        slope1[i, 144:272, :] = gelu_slope(xb2[1, 64:192, lanes].astype(F32))
        slope1[i, 272:288, :] = gelu_slope(halo1[1, :, lanes].astype(F32))

    each(1, 16, lambda step: d_copy(step).wait_recv())
    d_own.wait()
    shared = d_out[...].astype(F32) * rl[...]
    d_out[...] = shared.astype(BF16)
    dn[...] = jnp.transpose(shared).astype(BF16)
    delta[...] = jnp.sum(shared * attn[...], axis=0, keepdims=True)
    dk_acc[...] = jnp.zeros_like(dk_acc)

    def place_lanes(ref, number):
        return ref.at[:, pl.ds(pl.multiple_of(number * 128, 128), 128)]

    def grad_copy(held, landed, send, recv):
        def copy(step):
            to = lax.rem(chip + step, 16)
            return remote(place_lanes(held, to), landed.at[chip], send.at[step], recv.at[step], on_chip(to))

        return copy

    b_copy = grad_copy(dq_t, dq_recv, bs, br)
    c_copy = grad_copy(dk_t, dk_recv, cs, cr)
    v_copy = grad_copy(dv_t, dv_recv, vs, vr)

    def block_of(number):
        return lax.rem(chip // (QB // 128) + number, LENGTH // QB)

    def send_block(block, copy):
        for part in range(QB // 128):
            step = lax.rem(QB // 128 * block + part - chip + 16, 16)

            @pl.when(step > 0)
            def _():
                copy(step).start()

    def value_gradients(number):
        block = block_of(number)
        held = pl.ds(pl.multiple_of(block * QB, QB), QB)
        dv_t[:, held] = jnp.transpose(dot(e_mat[held, :], dn[...], NN)).astype(BF16)
        send_block(block, v_copy)

    each(0, LENGTH // QB, value_gradients)

    def gradients(number):
        block = block_of(number)
        lanes = pl.ds(pl.multiple_of(block * QB, QB), QB)
        moved = dot(vn[...], d_out[:, lanes], NN) - delta[:, lanes]
        slopes = (e_mat[:, lanes].astype(F32) * moved).astype(BF16)
        dq_t[:, lanes] = (dot(kt[...], slopes, NN) * SCALE).astype(BF16)
        send_block(block, b_copy)
        dk_acc[...] += dot(slopes, qn[lanes, :], NN)

    each(0, LENGTH // QB, gradients)
    dk_t[...] = jnp.transpose(dk_acc[...] * SCALE).astype(BF16)
    each(1, 16, lambda step: c_copy(step).start())
    own_copies = [
        pltpu.make_async_copy(place_lanes(held, chip), landed.at[chip], loc_sem.at[23 + i])
        for i, (held, landed) in enumerate(((dq_t, dq_recv), (dk_t, dk_recv), (dv_t, dv_recv)))
    ]
    for copy in own_copies:
        copy.start()

    for step in (1, 3, 2):
        slab_b.two(step).wait_recv()
        slab_b.cross(step).start()

    loaded(10)
    loaded(12)
    loaded(13)
    pre_two = jnp.concatenate([xb2[0, 0:64, :], xb2[1, 0:64, :]], axis=0).astype(F32)
    slope2 = gelu_slope(pre_two)
    layer_in = gelu_value(pre_two) + pair[0:1] * near[0] + pair[1:2] * near[1]
    center = jnp.mean(layer_in, axis=-1, keepdims=True)
    moved = layer_in - center
    rstd = 1.0 / jnp.sqrt(jnp.mean(moved * moved, axis=-1, keepdims=True) + 1e-05)
    normed = moved * rstd

    for step in range(4):
        slab_b.cross(step).wait_recv()

    def compact_b(number):
        slabs = slabs_of(wb, number)
        rows = pl.ds(pl.multiple_of(number * 80, 16), 80)
        for i in range(6):
            w_full[1 + i, rows, :] = jnp.concatenate(
                [slab[i * 40 : i * 40 + 40] for slab in slabs], axis=0
            ).astype(BF16)

    each(0, 8, compact_b)

    slab_b.sent()

    def sent(step):
        for copy in (u_copy, d_copy, b_copy, v_copy):
            copy(step).wait_send()

    each(1, 16, sent)
    for copy in (swap1, swap2, swap3, edge_up, edge_down):
        copy.wait_send()

    for copy in own_copies:
        copy.wait()
    for copy in (v_copy, b_copy, c_copy):
        each(1, 16, lambda step: copy(step).wait_recv())
    d_normed = jnp.zeros((128, WIDTH), F32)
    for i, ref in enumerate((dq_recv, dk_recv, dv_recv)):
        turned = jnp.concatenate([ref[head].astype(F32)[0:40] for head in range(16)], axis=0)
        d_normed = d_normed + dot(jnp.transpose(turned).astype(BF16), w_full[1 + i], NT)
    scaled = d_normed * gain[...].reshape(1, WIDTH)
    d_layer = rstd * (
        scaled
        - jnp.mean(scaled, axis=-1, keepdims=True)
        - normed * jnp.mean(scaled * normed, axis=-1, keepdims=True)
    )
    d2_buf[...] = ((up[...].reshape(128, WIDTH).astype(F32) + d_layer) * slope2).astype(BF16)
    row_up = remote(d2_buf.at[pl.ds(112, 16), :], halo2.at[0], hs.at[2], hr.at[2], after)
    row_down = remote(d2_buf.at[pl.ds(0, 16), :], halo2.at[1], hs.at[3], hr.at[3], before)
    row_up.start()
    row_down.start()
    each(1, 16, lambda step: c_copy(step).wait_send())
    row_up.wait_recv()
    row_down.wait_recv()
    has_before = jnp.where(chip > 0, 1.0, 0.0).astype(BF16)
    has_after = jnp.where(chip < 15, 1.0, 0.0).astype(BF16)
    rows = jnp.concatenate([halo2[0] * has_before, d2_buf[...], halo2[1] * has_after], axis=0)
    tap0, tap1, tap2 = (dot(rows, w_full[4 + i], NT) for i in range(3))
    even_slope = jnp.concatenate([slope1[i, pl.ds(16, 136, stride=2), :] for i in range(5)], axis=1)
    odd_slope = jnp.concatenate([slope1[i, pl.ds(1, 136, stride=2), :] for i in range(5)], axis=1)
    spot = lax.broadcasted_iota(jnp.int32, (136, 1), 0)
    even = tap1[16:152] * even_slope
    even = jnp.where((spot < 128) | (chip < 15), even, 0.0).astype(BF16)
    odd = (tap2[8:144] + tap0[9:145]) * odd_slope
    odd = jnp.where((spot >= 8) | (chip > 0), odd, 0.0).astype(BF16)
    even_mel = dot(even, w_last[...], NT)
    odd_mel = dot(odd, w_last[...], NT)
    mel_even = odd_mel[8:136, 0:128] + even_mel[0:128, 128:256] + odd_mel[7:135, 256:384]
    mel_odd = even_mel[1:129, 0:128] + odd_mel[8:136, 128:256] + even_mel[0:128, 256:384]
    for block in range(2):
        mel_buf[block, 0:64, :] = mel_even[block * 64 : block * 64 + 64]
        mel_buf[block, 64:128, :] = mel_odd[block * 64 : block * 64 + 64]
    swap4 = remote(mel_buf.at[other], mel_recv, xs.at[3], xr.at[3], sibling)
    swap4.start()
    for half in range(2):
        own = mel_buf[core, half * 64 : half * 64 + 64, :]
        out[pl.ds(2 * half + core, 64, stride=4), :] = own
    swap4.wait_recv()
    for half in range(2):
        out[pl.ds(2 * half + other, 64, stride=4), :] = mel_recv[half * 64 : half * 64 + 64, :]
    for copy in (swap4, row_up, row_down):
        copy.wait_send()


def per_device(
    frame_counts, dest_rank, grad_rows, queries, key_rows, value_rows, conv2_pre, conv1_pre,
    norm_gain, w_proj, w_out, w_qkv, w_conv2, w_conv1,
):
    chip_tab, near_tab = tables()
    target = jnp.transpose(dest_rank[0, :, :, 0])
    grads = jnp.transpose(grad_rows[0], (1, 0, 2)).reshape(192, HID)
    anywhere = pl.BlockSpec(memory_space=pl.ANY)
    vmem = pl.BlockSpec(memory_space=pltpu.VMEM)
    scratch = [
        ((2, 64), jnp.int32), ((WIDTH,), F32), ((2, WIDTH), F32),
        ((192, HID), BF16), ((64, 2, WIDTH), BF16), ((64, 2, WIDTH), BF16), ((64, 2, WIDTH), BF16),
        ((64, 2, WIDTH), BF16), ((128, 2, WIDTH), BF16), ((40, WIDTH), BF16), ((3, 40, WIDTH), BF16),
        ((3, 40, WIDTH), BF16), ((3, 8, WIDTH), BF16), ((2, 128, WIDTH), F32),
        ((64, WIDTH), BF16), ((256, WIDTH), BF16), ((WIDTH, HID), BF16), ((16, 64, WIDTH), BF16),
        ((16, 256, WIDTH), BF16), ((7, WIDTH, WIDTH), BF16), ((384, WIDTH), BF16),
        ((2, 192, WIDTH), BF16), ((2, 192, WIDTH), BF16), ((2, 192, WIDTH), BF16), ((2, 192, WIDTH), BF16),
        ((16, 128, 128), BF16), ((128, LENGTH), BF16), ((48, LENGTH), BF16), ((48, LENGTH), BF16), ((48, LENGTH), BF16),
        ((LENGTH, 48), BF16), ((LENGTH, 48), BF16), ((LENGTH, 48), BF16),
        ((16, 16, WIDTH), BF16), ((16, 16, WIDTH), BF16), ((2, 64, WIDTH), BF16), ((2, 64, WIDTH), BF16),
        ((16, 48, 128), BF16), ((48, LENGTH), BF16), ((LENGTH, 48), BF16),
        ((LENGTH, LENGTH), BF16), ((LENGTH, QB), F32), ((1, LENGTH), F32), ((1, LENGTH), F32),
        ((48, LENGTH), F32), ((LENGTH, 48), F32), ((48, LENGTH), BF16), ((48, LENGTH), BF16),
        ((48, LENGTH), BF16), ((16, 48, 128), BF16), ((16, 48, 128), BF16), ((16, 48, 128), BF16),
        ((5, 288, 128), F32), ((2, 16, WIDTH), BF16), ((128, WIDTH), BF16), ((2, 16, WIDTH), BF16),
        ((2, 128, 128), F32), ((128, 128), F32),
    ]
    sems = [26, 16] + [4] * 7 + [16, 2] + [4] * 6 + [16, 2] + [4] * 6 + [4, 4] + [16] * 12 + [4, 4]
    result = pl.pallas_call(
        kernel,
        out_shape=jax.ShapeDtypeStruct((256, 128), F32),
        in_specs=[pl.BlockSpec(memory_space=pltpu.SMEM)] + [anywhere] * 15,
        out_specs=vmem,
        scratch_shapes=[pltpu.VMEM(shape, kind) for shape, kind in scratch]
        + [pltpu.SemaphoreType.DMA((n,)) for n in sems],
        compiler_params=pltpu.CompilerParams(
            collective_id=0, has_side_effects=True, vmem_limit_bytes=58 << 20
        ),
    )(
        frame_counts, target, grads, queries, key_rows, value_rows, conv2_pre, conv1_pre,
        norm_gain, w_proj, w_out, w_qkv, w_conv2, w_conv1,
        jnp.asarray(chip_tab), jnp.asarray(near_tab),
    )
    return result.reshape(1, 128, 2, 128)


def solution(mesh):
    rows = P("llm", "enc", None, None)
    placed = (
        P("llm", None), rows, P("llm", None, "enc", None), rows, rows, rows, rows, rows, P(),
        P(None, "llm"), P("llm", None), P(None, "llm", None), P(None, "llm", None), P(None, "llm", None),
    )
    return jax.shard_map(
        per_device, mesh=mesh, in_specs=placed, out_specs=rows, check_vma=False
    )
```

```python
import functools

import jax
import jax.numpy as jnp
import numpy as np
from jax import lax
from jax.experimental import pallas as pl
from jax.experimental.pallas import tpu as pltpu
from jax.sharding import PartitionSpec as P

MESH = pl.DeviceIdType.MESH
F32, BF16 = jnp.float32, jnp.bfloat16
HEAD_DIM = 40
WIDTH = 640
HID = 2048
LENGTH = 2048
SCALE = HEAD_DIM ** (-0.5)
LOG2E = 1.4426950408889634
MASKED = -1e30
ROOT_HALF = 0.7071067811865476
INV_ROOT_TWO_PI = 0.3989422804014327
QB = 512


def gelu_value(value):
    return value * 0.5 * (1.0 + lax.erf(value * ROOT_HALF))


def gelu_slope(value):
    return (
        0.5 * (1.0 + lax.erf(value * ROOT_HALF))
        + value * jnp.exp(-0.5 * value * value) * INV_ROOT_TWO_PI
    )


def dot(a, b, dims):
    return lax.dot_general(a, b, (dims, ((), ())), preferred_element_type=F32)


NN = ((1,), (0,))
NT = ((1,), (1,))
TN = ((0,), (0,))


def tables():
    inverse = 10000.0 ** (-np.arange(320) / 319.0)
    base = 128.0 * np.arange(16)[:, None] * inverse[None, :]
    local = np.arange(128.0)[:, None] * inverse[None, :]
    first = np.concatenate([np.sin(base), np.cos(base)], axis=1)
    second = np.concatenate([np.cos(base), -np.sin(base)], axis=1)
    chip = np.stack([first, second], axis=1).astype(np.float32)
    near = np.stack(
        [np.concatenate([np.cos(local)] * 2, 1), np.concatenate([np.sin(local)] * 2, 1)]
    ).astype(np.float32)
    return chip, near


def kernel(
    counts, target_in, grads, q_in, k_in, v_in, c2_in, c1_in, gain_in, wp_in, wo_in, wqkv_in, wc2_in, wc1_in,
    chip_tab, near_tab,
    out,
    target, gain, pair, g_loc, q_loc, k_loc, v_loc, c2_loc, c1_loc, wo_loc, wqkv_loc, wc2_loc, wc1_loc, near,
    a_slab, b_slab, wp, wa, wb, w_full, w_last,
    cl1, cl2, xb1, xb2, head_send, qkv, qt, kt, vt, kn, vn, qn,
    u_send, u_recv, up_send, up, d_send, d_out, dn,
    e_mat, big, rl, delta, attn, dk_acc, dq_t, dk_t, dv_t, dq_recv, dk_recv, dv_recv,
    slope1, halo1, d2_buf, halo2, mel_buf, mel_recv,
    loc_sem, wpz_s, wpz_r, wp1_s, wp1_r, wp2_s, wp2_r, wpc_s, wpc_r,
    waz_s, waz_r, wa1_s, wa1_r, wa2_s, wa2_r, wac_s, wac_r,
    wbz_s, wbz_r, wb1_s, wb1_r, wb2_s, wb2_r, wbc_s, wbc_r,
    xs, xr, qs, qr, us, ur, ds_, dr, bs, br, cs, cr, vs, vr, hs, hr,
):
    z = lax.axis_index("llm")
    e = lax.axis_index("enc")
    core = lax.rem(e, 2)
    other = 1 - core
    chip = e // 2
    x = lax.rem(chip, 4)
    y = chip // 4
    a = jnp.where(core == 0, x, y)
    b = jnp.where(core == 0, y, x)
    sibling = (z, chip * 2 + other)

    def along_a(step):
        to = lax.rem(a + step, 4)
        return (z, jnp.where(core == 0, y * 4 + to, to * 4 + x) * 2 + core)

    def along_b(step):
        to = lax.rem(b + step, 4)
        return (z, jnp.where(core == 0, to * 4 + x, y * 4 + to) * 2 + core)

    def along_z(step):
        return (lax.rem(z + step, 16), e)

    def on_chip(number):
        return (z, number * 2 + core)

    def remote(src, dst, send, recv, device):
        return pltpu.make_async_remote_copy(
            src_ref=src, dst_ref=dst, send_sem=send, recv_sem=recv, device_id=device, device_id_type=MESH
        )

    def each(low, high, act):
        def body(step, carry):
            act(step)
            return carry

        lax.fori_loop(low, high, body, 0)

    barrier = pltpu.get_barrier_semaphore()

    def greet(step):
        pl.semaphore_signal(barrier, inc=1, device_id=along_z(step), device_id_type=MESH)
        pl.semaphore_signal(
            barrier, inc=1, device_id=on_chip(lax.rem(chip + step, 16)), device_id_type=MESH
        )

    each(1, 16, greet)
    pl.semaphore_signal(barrier, inc=1, device_id=sibling, device_id_type=MESH)

    loads = [
        (q_in.at[0], q_loc), (k_in.at[0], k_loc), (v_in.at[0], v_loc), (wo_in, wo_loc), (wc1_in, wc1_loc),
        (wqkv_in, wqkv_loc), (wc2_in, wc2_loc), (c2_in.at[0], c2_loc), (c1_in.at[0], c1_loc),
        (grads, g_loc), (near_tab, near), (target_in, target), (gain_in, gain), (chip_tab.at[chip], pair),
    ]
    for i, (src, dst) in enumerate(loads):
        pltpu.make_async_copy(src, dst, loc_sem.at[i]).start()

    def loaded(i):
        pltpu.make_async_copy(loads[i][0], loads[i][1], loc_sem.at[i]).wait()

    pl.semaphore_wait(barrier, 31)

    piece = 2 * b + a // 2
    kind = lax.rem(a, 2) + 2 * core
    wp_rows = pl.ds(pl.multiple_of(piece * 80, 16), 80)

    def wpz(step, index):
        return remote(
            wp_in.at[wp_rows, :],
            wp.at[wp_rows, pl.ds(pl.multiple_of((kind * 4 + index) * 128, 128), 128)],
            wpz_s.at[step], wpz_r.at[index], along_z(step),
        )

    wp_sends = lax.rem(z, 4) == kind
    wp_own = pltpu.make_async_copy(
        wp_in.at[wp_rows, :],
        wp.at[wp_rows, pl.ds(pl.multiple_of((kind * 4 + z // 4) * 128, 128), 128)],
        loc_sem.at[14],
    )

    @pl.when(wp_sends)
    def _():
        each(1, 16, lambda step: wpz(step, z // 4).start())
        wp_own.start()

    for i, ref in enumerate((q_loc, k_loc, v_loc)):
        loaded(i)
        for clip in range(2):
            cl1[clip, i * 64 : (i + 1) * 64, :] = ref[:, clip, :]
    swap1 = remote(cl1.at[other], xb1.at[core], xs.at[0], xr.at[0], sibling)
    swap1.start()
    keep1 = pltpu.make_async_copy(cl1.at[core], xb1.at[core], loc_sem.at[15])
    keep1.start()

    for index in range(4):
        @pl.when(kind + 4 * index != z)
        def _():
            wpz(1, index).wait_recv()

    @pl.when(wp_sends)
    def _():
        wp_own.wait()

    def wp1(step):
        block = wp.at[wp_rows, pl.ds(pl.multiple_of(kind * 512, 128), 512)]
        return remote(block, block, wp1_s.at[step], wp1_r.at[step], along_a(step))

    for step in range(1, 4):
        wp1(step).start()

    group8 = a + 4 * core

    class Slab:
        def __init__(self, rows, held, full, sems, own_sem):
            self.rows, self.held, self.full = rows, held, full
            self.zs, self.zr, self.s1, self.r1, self.s2, self.r2, self.s3, self.r3 = sems
            self.part = pl.ds(pl.multiple_of(b * rows, 16), rows)
            self.sends = lax.rem(z, 8) == group8
            self.own = pltpu.make_async_copy(
                held.at[self.part, :], full.at[group8 * 2 + z // 8, self.part, :], own_sem
            )

        def deep(self, step, index):
            return remote(
                self.held.at[self.part, :], self.full.at[group8 * 2 + index, self.part, :],
                self.zs.at[step], self.zr.at[index], along_z(step),
            )

        def start_deep(self):
            @pl.when(self.sends)
            def _():
                each(1, 16, lambda step: self.deep(step, z // 8).start())
                self.own.start()

        def wait_deep(self):
            for index in range(2):
                @pl.when(group8 + 8 * index != z)
                def _():
                    self.deep(1, index).wait_recv()

            @pl.when(self.sends)
            def _():
                self.own.wait()

        def one(self, step):
            block = self.full.at[pl.ds(group8 * 2, 2), self.part, :]
            return remote(block, block, self.s1.at[step], self.r1.at[step], along_a(step))

        def band(self, number):
            return self.full.at[
                pl.ds(core * 8, 8), pl.ds(pl.multiple_of(number * self.rows, 16), self.rows), :
            ]

        def two(self, step):
            return remote(self.band(b), self.band(b), self.s2.at[step], self.r2.at[step], along_b(step))

        def cross(self, step):
            band = self.band(lax.rem(b - step + 4, 4))
            return remote(band, band, self.s3.at[step], self.r3.at[step], sibling)

        def sent(self):
            @pl.when(self.sends)
            def _():
                each(1, 16, lambda step: self.deep(step, z // 8).wait_send())

            for step in range(1, 4):
                self.one(step).wait_send()
                self.two(step).wait_send()
            for step in range(4):
                self.cross(step).wait_send()

    slab_a = Slab(
        16, a_slab, wa, (waz_s, waz_r, wa1_s, wa1_r, wa2_s, wa2_r, wac_s, wac_r), loc_sem.at[16]
    )
    slab_b = Slab(
        64, b_slab, wb, (wbz_s, wbz_r, wb1_s, wb1_r, wb2_s, wb2_r, wbc_s, wbc_r), loc_sem.at[17]
    )
    loaded(3)
    loaded(4)
    parts = [wo_loc[...].astype(F32)] + [wc1_loc[i].astype(F32) for i in range(3)]
    a_slab[...] = jnp.concatenate(parts, axis=0).astype(BF16)
    slab_a.start_deep()
    loaded(5)
    loaded(6)
    parts = [wqkv_loc[i].astype(F32) for i in range(3)] + [wc2_loc[i].astype(F32) for i in range(3)]
    b_slab[...] = jnp.concatenate(parts + [jnp.zeros((16, WIDTH), F32)], axis=0).astype(BF16)
    slab_b.start_deep()

    swap1.wait_recv()
    keep1.wait()
    zero_rows = jnp.zeros((8, 128), F32)
    turned = []
    for i in range(3):
        rows = jnp.concatenate(
            [xb1[0, i * 64 : (i + 1) * 64, :], xb1[1, i * 64 : (i + 1) * 64, :]], axis=0
        ).astype(F32)
        turned.append(jnp.transpose(rows))
    for head in range(16):
        head_send[head] = jnp.concatenate(
            [part[head * 40 : head * 40 + 40] for part in turned] + [zero_rows], axis=0
        ).astype(BF16)
    chip_lanes = pl.ds(pl.multiple_of(chip * 128, 128), 128)

    def qkv_copy(step):
        to = lax.rem(chip + step, 16)
        return remote(head_send.at[to], qkv.at[:, chip_lanes], qs.at[step], qr.at[step], on_chip(to))

    each(1, 16, lambda step: qkv_copy(step).start())
    qkv_own = pltpu.make_async_copy(head_send.at[chip], qkv.at[:, chip_lanes], loc_sem.at[18])
    qkv_own.start()

    for step in range(1, 4):
        wp1(step).wait_recv()

    def wp_set(number):
        return wp.at[
            pl.ds(pl.multiple_of(number * 160, 16), 160), pl.ds(pl.multiple_of(core * 1024, 128), 1024)
        ]

    def wp2(step):
        return remote(wp_set(b), wp_set(b), wp2_s.at[step], wp2_r.at[step], along_b(step))

    def wpc(step):
        held = wp_set(lax.rem(b - step + 4, 4))
        return remote(held, held, wpc_s.at[step], wpc_r.at[step], sibling)

    for step in (2, 1, 3):
        wp2(step).start()
    wpc(0).start()

    for step in (1, 3, 2):
        wp2(step).wait_recv()
        wpc(step).start()

    slab_a.wait_deep()
    for step in range(1, 4):
        slab_a.one(step).start()

    loaded(9)
    for step in range(4):
        wpc(step).wait_recv()

    total = jnp.zeros((192, WIDTH), F32)
    for number in range(4):
        rows = jnp.concatenate(
            [g_loc[:, (number + 4 * i) * 128 : (number + 4 * i + 1) * 128] for i in range(4)], axis=1
        )
        total = total + dot(rows, wp[:, number * 512 : (number + 1) * 512], NT)
    slot_row = lax.broadcasted_iota(jnp.int32, (256, 192), 0)
    held_row = lax.broadcasted_iota(jnp.int32, (256, 192), 1)
    order = (lax.rem(slot_row, 16) * 16 + slot_row // 16 == held_row).astype(F32).astype(BF16)
    u_send[...] = dot(order, total.astype(BF16), NN).astype(BF16).reshape(16, 16, WIDTH)

    def u_copy(step):
        to = lax.rem(z + step, 16)
        return remote(u_send.at[to], u_recv.at[z], us.at[step], ur.at[step], (to, e))

    each(1, 16, lambda step: u_copy(step).start())
    u_own = pltpu.make_async_copy(u_send.at[z], u_recv.at[z], loc_sem.at[19])
    u_own.start()

    loaded(7)
    loaded(8)
    for clip in range(2):
        cl2[clip, 0:64, :] = c2_loc[:, clip, :]
        cl2[clip, 64:192, :] = c1_loc[:, clip, :]
    swap2 = remote(cl2.at[other], xb2.at[core], xs.at[1], xr.at[1], sibling)
    swap2.start()
    keep2 = pltpu.make_async_copy(cl2.at[core], xb2.at[core], loc_sem.at[20])
    keep2.start()

    for step in range(1, 4):
        slab_a.one(step).wait_recv()
    for step in (2, 1, 3):
        slab_a.two(step).start()
    slab_a.cross(0).start()
    slab_b.wait_deep()
    for step in range(1, 4):
        slab_b.one(step).start()

    swap2.wait_recv()
    keep2.wait()
    after = on_chip(lax.rem(chip + 1, 16))
    before = on_chip(lax.rem(chip + 15, 16))
    edge_up = remote(xb2.at[1, pl.ds(176, 16), :], halo1.at[0], hs.at[0], hr.at[0], after)
    edge_down = remote(xb2.at[0, pl.ds(64, 16), :], halo1.at[1], hs.at[1], hr.at[1], before)
    edge_up.start()
    edge_down.start()

    each(1, 16, lambda step: qkv_copy(step).wait_recv())
    qkv_own.wait()
    row8 = lax.broadcasted_iota(jnp.int32, (8, LENGTH), 0)
    places = lax.broadcasted_iota(jnp.int32, (8, LENGTH), 1)
    own_count = jnp.where(core == 0, counts[0, 0], counts[0, 1])
    ones_rows = jnp.where(row8 == 0, 1.0, 0.0)
    bias_rows = jnp.where((row8 == 0) & (places >= own_count), MASKED, 0.0)
    arrived = qkv[...].astype(F32)
    wide_q = jnp.concatenate([arrived[0:40], ones_rows], axis=0)
    wide_k = jnp.concatenate([arrived[40:80], bias_rows], axis=0)
    wide_v = arrived[80:128]
    qt[...] = wide_q.astype(BF16)
    kt[...] = wide_k.astype(BF16)
    vt[...] = wide_v.astype(BF16)
    qn[...] = jnp.transpose(wide_q).astype(BF16)
    kn[...] = jnp.transpose(wide_k).astype(BF16)
    vn[...] = jnp.transpose(wide_v).astype(BF16)

    def exponentials(number):
        lanes = pl.ds(pl.multiple_of(number * QB, QB), QB)
        big[...] = dot(kn[...], qt[:, lanes], NN)
        highest = jnp.max(big[...], axis=0, keepdims=True)
        weights = jnp.exp2((big[...] - highest) * (SCALE * LOG2E))
        weights_b = weights.astype(BF16)
        e_mat[:, lanes] = weights_b
        share = 1.0 / jnp.sum(weights, axis=0, keepdims=True)
        rl[:, lanes] = share
        attn[:, lanes] = dot(vt[...], weights_b, NN) * share

    each(0, LENGTH // QB, exponentials)

    for step in (1, 3, 2):
        slab_a.two(step).wait_recv()
        slab_a.cross(step).start()
    for step in range(1, 4):
        slab_b.one(step).wait_recv()
    for step in (2, 1, 3):
        slab_b.two(step).start()
    slab_b.cross(0).start()
    for step in range(4):
        slab_a.cross(step).wait_recv()

    def slabs_of(full, number):
        return [full[lax.rem(place, 8) * 2 + place // 8].astype(F32) for place in (2 * number, 2 * number + 1)]

    def compact_a(number):
        slabs = slabs_of(wa, number)
        rows = pl.ds(pl.multiple_of(number * 80, 16), 80)
        w_full[0, rows, :] = jnp.concatenate([slab[0:40] for slab in slabs], axis=0).astype(BF16)
        for i in range(3):
            w_last[pl.ds(pl.multiple_of(i * 128 + number * 16, 16), 16), :] = jnp.concatenate(
                [slab[40 + i * 8 : 48 + i * 8] for slab in slabs], axis=0
            ).astype(BF16)

    each(0, 8, compact_a)

    loaded(11)
    slots = lax.broadcasted_iota(jnp.int32, (256, 64), 0)
    frame = e * 64 + lax.broadcasted_iota(jnp.int32, (256, 64), 1)
    named = []
    for clip in range(2):
        hit = (target[clip : clip + 1, :] == slots // 16) & (frame < counts[0, clip])
        named.append(jnp.where(hit, 1.0, 0.0))
    earlier = lax.broadcasted_iota(jnp.int32, (64, 64), 0)
    later = lax.broadcasted_iota(jnp.int32, (64, 64), 1)
    upto = (earlier <= later).astype(F32).astype(BF16)
    under = (earlier < later).astype(F32).astype(BF16)
    named_b = [part.astype(BF16) for part in named]
    seen = [
        dot(named_b[0], upto, NN) + dot(named_b[1], under, NN),
        dot(named_b[0], upto, NN) + dot(named_b[1], upto, NN),
    ]
    within = lax.rem(slots, 16).astype(F32) + 1.0
    choose = jnp.transpose(
        jnp.concatenate([jnp.where(seen[i] == within, named[i], 0.0) for i in range(2)], axis=1)
    ).astype(BF16)

    @pl.when(wp_sends)
    def _():
        each(1, 16, lambda step: wpz(step, z // 4).wait_send())

    for step in range(1, 4):
        for copy in (wp1, wp2, wpc):
            copy(step).wait_send()
    wpc(0).wait_send()
    slab_a.sent()
    each(1, 16, lambda step: qkv_copy(step).wait_send())

    each(1, 16, lambda step: u_copy(step).wait_recv())
    u_own.wait()
    up_send[...] = (
        dot(choose, u_recv[...].reshape(256, WIDTH), NN).astype(BF16).reshape(2, 64, WIDTH)
    )
    swap3 = remote(up_send.at[other], up.at[core], xs.at[2], xr.at[2], sibling)
    swap3.start()
    keep3 = pltpu.make_async_copy(up_send.at[core], up.at[core], loc_sem.at[21])
    keep3.start()
    swap3.wait_recv()
    keep3.wait()
    d_attn = dot(w_full[0], up[...].reshape(128, WIDTH), NT)
    for head in range(16):
        d_send[head] = jnp.concatenate([d_attn[head * 40 : head * 40 + 40], zero_rows], axis=0).astype(
            BF16
        )

    def d_copy(step):
        to = lax.rem(chip + step, 16)
        return remote(d_send.at[to], d_out.at[:, chip_lanes], ds_.at[step], dr.at[step], on_chip(to))

    each(1, 16, lambda step: d_copy(step).start())
    d_own = pltpu.make_async_copy(d_send.at[chip], d_out.at[:, chip_lanes], loc_sem.at[22])
    d_own.start()

    edge_up.wait_recv()
    edge_down.wait_recv()
    for i in range(5):
        lanes = slice(i * 128, i * 128 + 128)
        slope1[i, 0:16, :] = gelu_slope(halo1[0, :, lanes].astype(F32))
        slope1[i, 16:144, :] = gelu_slope(xb2[0, 64:192, lanes].astype(F32))
        slope1[i, 144:272, :] = gelu_slope(xb2[1, 64:192, lanes].astype(F32))
        slope1[i, 272:288, :] = gelu_slope(halo1[1, :, lanes].astype(F32))

    each(1, 16, lambda step: d_copy(step).wait_recv())
    d_own.wait()
    shared = d_out[...].astype(F32) * rl[...]
    d_out[...] = shared.astype(BF16)
    dn[...] = jnp.transpose(shared).astype(BF16)
    delta[...] = jnp.sum(shared * attn[...], axis=0, keepdims=True)
    dk_acc[...] = jnp.zeros_like(dk_acc)

    def place_lanes(ref, number):
        return ref.at[:, pl.ds(pl.multiple_of(number * 128, 128), 128)]

    def grad_copy(held, landed, send, recv):
        def copy(step):
            to = lax.rem(chip + step, 16)
            return remote(place_lanes(held, to), landed.at[chip], send.at[step], recv.at[step], on_chip(to))

        return copy

    b_copy = grad_copy(dq_t, dq_recv, bs, br)
    c_copy = grad_copy(dk_t, dk_recv, cs, cr)
    v_copy = grad_copy(dv_t, dv_recv, vs, vr)

    def block_of(number):
        return lax.rem(chip // (QB // 128) + number, LENGTH // QB)

    def send_block(block, copy):
        for part in range(QB // 128):
            step = lax.rem(QB // 128 * block + part - chip + 16, 16)

            @pl.when(step > 0)
            def _():
                copy(step).start()

    def value_gradients(number):
        block = block_of(number)
        held = pl.ds(pl.multiple_of(block * QB, QB), QB)
        dv_t[:, held] = jnp.transpose(dot(e_mat[held, :], dn[...], NN)).astype(BF16)
        send_block(block, v_copy)

    each(0, LENGTH // QB, value_gradients)

    def gradients(number):
        block = block_of(number)
        lanes = pl.ds(pl.multiple_of(block * QB, QB), QB)
        moved = dot(vn[...], d_out[:, lanes], NN) - delta[:, lanes]
        slopes = (e_mat[:, lanes].astype(F32) * moved).astype(BF16)
        dq_t[:, lanes] = (dot(kt[...], slopes, NN) * SCALE).astype(BF16)
        send_block(block, b_copy)
        dk_acc[...] += dot(slopes, qn[lanes, :], NN)

    each(0, LENGTH // QB, gradients)
    dk_t[...] = jnp.transpose(dk_acc[...] * SCALE).astype(BF16)
    each(1, 16, lambda step: c_copy(step).start())
    own_copies = [
        pltpu.make_async_copy(place_lanes(held, chip), landed.at[chip], loc_sem.at[23 + i])
        for i, (held, landed) in enumerate(((dq_t, dq_recv), (dk_t, dk_recv), (dv_t, dv_recv)))
    ]
    for copy in own_copies:
        copy.start()

    for step in (1, 3, 2):
        slab_b.two(step).wait_recv()
        slab_b.cross(step).start()

    loaded(10)
    loaded(12)
    loaded(13)
    pre_two = jnp.concatenate([xb2[0, 0:64, :], xb2[1, 0:64, :]], axis=0).astype(F32)
    slope2 = gelu_slope(pre_two)
    layer_in = gelu_value(pre_two) + pair[0:1] * near[0] + pair[1:2] * near[1]
    center = jnp.mean(layer_in, axis=-1, keepdims=True)
    moved = layer_in - center
    rstd = 1.0 / jnp.sqrt(jnp.mean(moved * moved, axis=-1, keepdims=True) + 1e-05)
    normed = moved * rstd

    for step in range(4):
        slab_b.cross(step).wait_recv()

    def compact_b(number):
        slabs = slabs_of(wb, number)
        rows = pl.ds(pl.multiple_of(number * 80, 16), 80)
        for i in range(6):
            w_full[1 + i, rows, :] = jnp.concatenate(
                [slab[i * 40 : i * 40 + 40] for slab in slabs], axis=0
            ).astype(BF16)

    each(0, 8, compact_b)

    slab_b.sent()

    def sent(step):
        for copy in (u_copy, d_copy, b_copy, v_copy):
            copy(step).wait_send()

    each(1, 16, sent)
    for copy in (swap1, swap2, swap3, edge_up, edge_down):
        copy.wait_send()

    for copy in own_copies:
        copy.wait()
    for copy in (v_copy, b_copy, c_copy):
        each(1, 16, lambda step: copy(step).wait_recv())
    d_normed = jnp.zeros((128, WIDTH), F32)
    for i, ref in enumerate((dq_recv, dk_recv, dv_recv)):
        turned = jnp.concatenate([ref[head].astype(F32)[0:40] for head in range(16)], axis=0)
        d_normed = d_normed + dot(jnp.transpose(turned).astype(BF16), w_full[1 + i], NT)
    scaled = d_normed * gain[...].reshape(1, WIDTH)
    d_layer = rstd * (
        scaled
        - jnp.mean(scaled, axis=-1, keepdims=True)
        - normed * jnp.mean(scaled * normed, axis=-1, keepdims=True)
    )
    d2_buf[...] = ((up[...].reshape(128, WIDTH).astype(F32) + d_layer) * slope2).astype(BF16)
    row_up = remote(d2_buf.at[pl.ds(112, 16), :], halo2.at[0], hs.at[2], hr.at[2], after)
    row_down = remote(d2_buf.at[pl.ds(0, 16), :], halo2.at[1], hs.at[3], hr.at[3], before)
    row_up.start()
    row_down.start()
    each(1, 16, lambda step: c_copy(step).wait_send())
    row_up.wait_recv()
    row_down.wait_recv()
    has_before = jnp.where(chip > 0, 1.0, 0.0).astype(BF16)
    has_after = jnp.where(chip < 15, 1.0, 0.0).astype(BF16)
    rows = jnp.concatenate([halo2[0] * has_before, d2_buf[...], halo2[1] * has_after], axis=0)
    tap0, tap1, tap2 = (dot(rows, w_full[4 + i], NT) for i in range(3))
    even_slope = jnp.concatenate([slope1[i, pl.ds(16, 136, stride=2), :] for i in range(5)], axis=1)
    odd_slope = jnp.concatenate([slope1[i, pl.ds(1, 136, stride=2), :] for i in range(5)], axis=1)
    spot = lax.broadcasted_iota(jnp.int32, (136, 1), 0)
    even = tap1[16:152] * even_slope
    even = jnp.where((spot < 128) | (chip < 15), even, 0.0).astype(BF16)
    odd = (tap2[8:144] + tap0[9:145]) * odd_slope
    odd = jnp.where((spot >= 8) | (chip > 0), odd, 0.0).astype(BF16)
    even_mel = dot(even, w_last[...], NT)
    odd_mel = dot(odd, w_last[...], NT)
    mel_even = odd_mel[8:136, 0:128] + even_mel[0:128, 128:256] + odd_mel[7:135, 256:384]
    mel_odd = even_mel[1:129, 0:128] + odd_mel[8:136, 128:256] + even_mel[0:128, 256:384]
    for block in range(2):
        mel_buf[block, 0:64, :] = mel_even[block * 64 : block * 64 + 64]
        mel_buf[block, 64:128, :] = mel_odd[block * 64 : block * 64 + 64]
    swap4 = remote(mel_buf.at[other], mel_recv, xs.at[3], xr.at[3], sibling)
    swap4.start()
    for half in range(2):
        own = mel_buf[core, half * 64 : half * 64 + 64, :]
        out[pl.ds(2 * half + core, 64, stride=4), :] = own
    swap4.wait_recv()
    for half in range(2):
        out[pl.ds(2 * half + other, 64, stride=4), :] = mel_recv[half * 64 : half * 64 + 64, :]
    for copy in (swap4, row_up, row_down):
        copy.wait_send()


def per_device(
    frame_counts, dest_rank, grad_rows, queries, key_rows, value_rows, conv2_pre, conv1_pre,
    norm_gain, w_proj, w_out, w_qkv, w_conv2, w_conv1,
):
    chip_tab, near_tab = tables()
    target = jnp.transpose(dest_rank[0, :, :, 0])
    grads = jnp.transpose(grad_rows[0], (1, 0, 2)).reshape(192, HID)
    anywhere = pl.BlockSpec(memory_space=pl.ANY)
    vmem = pl.BlockSpec(memory_space=pltpu.VMEM)
    scratch = [
        ((2, 64), jnp.int32), ((WIDTH,), F32), ((2, WIDTH), F32),
        ((192, HID), BF16), ((64, 2, WIDTH), BF16), ((64, 2, WIDTH), BF16), ((64, 2, WIDTH), BF16),
        ((64, 2, WIDTH), BF16), ((128, 2, WIDTH), BF16), ((40, WIDTH), BF16), ((3, 40, WIDTH), BF16),
        ((3, 40, WIDTH), BF16), ((3, 8, WIDTH), BF16), ((2, 128, WIDTH), F32),
        ((64, WIDTH), BF16), ((256, WIDTH), BF16), ((WIDTH, HID), BF16), ((16, 64, WIDTH), BF16),
        ((16, 256, WIDTH), BF16), ((7, WIDTH, WIDTH), BF16), ((384, WIDTH), BF16),
        ((2, 192, WIDTH), BF16), ((2, 192, WIDTH), BF16), ((2, 192, WIDTH), BF16), ((2, 192, WIDTH), BF16),
        ((16, 128, 128), BF16), ((128, LENGTH), BF16), ((48, LENGTH), BF16), ((48, LENGTH), BF16), ((48, LENGTH), BF16),
        ((LENGTH, 48), BF16), ((LENGTH, 48), BF16), ((LENGTH, 48), BF16),
        ((16, 16, WIDTH), BF16), ((16, 16, WIDTH), BF16), ((2, 64, WIDTH), BF16), ((2, 64, WIDTH), BF16),
        ((16, 48, 128), BF16), ((48, LENGTH), BF16), ((LENGTH, 48), BF16),
        ((LENGTH, LENGTH), BF16), ((LENGTH, QB), F32), ((1, LENGTH), F32), ((1, LENGTH), F32),
        ((48, LENGTH), F32), ((LENGTH, 48), F32), ((48, LENGTH), BF16), ((48, LENGTH), BF16),
        ((48, LENGTH), BF16), ((16, 48, 128), BF16), ((16, 48, 128), BF16), ((16, 48, 128), BF16),
        ((5, 288, 128), F32), ((2, 16, WIDTH), BF16), ((128, WIDTH), BF16), ((2, 16, WIDTH), BF16),
        ((2, 128, 128), F32), ((128, 128), F32),
    ]
    sems = [26, 16] + [4] * 7 + [16, 2] + [4] * 6 + [16, 2] + [4] * 6 + [4, 4] + [16] * 12 + [4, 4]
    result = pl.pallas_call(
        kernel,
        out_shape=jax.ShapeDtypeStruct((256, 128), F32),
        in_specs=[pl.BlockSpec(memory_space=pltpu.SMEM)] + [anywhere] * 15,
        out_specs=vmem,
        scratch_shapes=[pltpu.VMEM(shape, kind) for shape, kind in scratch]
        + [pltpu.SemaphoreType.DMA((n,)) for n in sems],
        compiler_params=pltpu.CompilerParams(
            collective_id=0, has_side_effects=True, vmem_limit_bytes=58 << 20
        ),
    )(
        frame_counts, target, grads, queries, key_rows, value_rows, conv2_pre, conv1_pre,
        norm_gain, w_proj, w_out, w_qkv, w_conv2, w_conv1,
        jnp.asarray(chip_tab), jnp.asarray(near_tab),
    )
    return result.reshape(1, 128, 2, 128)


def solution(mesh):
    rows = P("llm", "enc", None, None)
    placed = (
        P("llm", None), rows, P("llm", None, "enc", None), rows, rows, rows, rows, rows, P(),
        P(None, "llm"), P("llm", None), P(None, "llm", None), P(None, "llm", None), P(None, "llm", None),
    )
    return jax.shard_map(
        per_device, mesh=mesh, in_specs=placed, out_specs=rows, check_vma=False
    )
```
